256 devices in a mesh: doc: 2 (over y_hi), outer: 16 (over z, y_lo), inner: 8 (over x, core).
Axes of the slice: x: 4, y: 4 (y_hi: 2, y_lo: 2; y = y_hi * 2 + y_lo), z: 8, core: 2. Of those that a mesh axis runs over, the one named last changes fastest.
Arguments:
- tokens: bfloat16 [2, 16384, 12288], P('doc', ('outer', 'inner')), may hold values from -8 to 8
- qkv_weight: bfloat16 [12288, 768], P('outer', 'doc'), may hold values from -1 to 1
- span_pos: int32 [256], replicated, may hold values from 0 to 255, each once
Outputs:
- features: bfloat16 [2, 16384, 512], P('doc', ('outer', 'inner'))
The draws below stay inside these ranges and needn't reach their ends.
Inputs may be any that keep to these rules, and one draw needn't show every extreme that they name: `span_pos`: a permutation of the 256 block indices.
All inputs are finite; a program needn't handle non-finite values.
Results may differ from the reference program's by a relative error of at most 0.03.
Values may be sent and summed in bfloat16 or wider, within the bound.
A program may use at most 128 MiB of HBM per device.

```python
import math
import jax
import jax.numpy as jnp
from jax import lax

D = 12288
HD = 128
QH = 4
CH = 64
NCHUNK = 256
L = 16384
DOCS = 2
COLS = 768


def draw_tokens(key, part):
    key = jax.random.fold_in(key, 3)
    keys = jax.random.split(key, 1)
    return jnp.clip(jax.random.normal(keys[0], (DOCS, L, D), jnp.float32), -6.0, 6.0).astype(jnp.bfloat16)


def draw_qkv_weight(key, part):
    key = jax.random.fold_in(key, 5)
    spread = D ** (-0.5)
    return (jnp.clip(jax.random.normal(key, (D, COLS), jnp.float32), -6.0, 6.0) * spread).astype(jnp.bfloat16)


def setup_inputs(seed: int = 0) -> dict:
    arg_keys = jax.random.split(jax.random.key(seed), 4)
    tokens = draw_tokens(jax.random.fold_in(arg_keys[3], 71), 0)
    qkv_weight = draw_qkv_weight(jax.random.fold_in(arg_keys[3], 71), 0)
    span_pos = jax.random.permutation(arg_keys[2], NCHUNK).astype(jnp.int32)
    return dict(tokens=tokens, qkv_weight=qkv_weight, span_pos=span_pos)


def rope_tables(positions):
    half = HD // 2
    freq = 1000000.0 ** (-jnp.arange(half, dtype=jnp.float32) * 2.0 / HD)
    angle = positions.astype(jnp.float32)[:, None] * freq[None, :]
    return jnp.cos(angle), jnp.sin(angle)


def rotate(values, cosine, sine):
    half = HD // 2
    first = values[..., :half]
    second = values[..., half:]
    return jnp.concatenate([first * cosine - second * sine, second * cosine + first * sine], axis=-1)


def one_document(x_doc, qkv_weight, positions):
    proj = jnp.dot(x_doc, qkv_weight, preferred_element_type=jnp.float32)
    cosine, sine = rope_tables(positions)
    query = proj[:, :QH * HD].reshape(-1, QH, HD)
    query = (rotate(query, cosine[:, None, :], sine[:, None, :]) * (HD ** -0.5)).astype(jnp.bfloat16)
    key = rotate(proj[:, QH * HD:(QH + 1) * HD], cosine, sine).astype(jnp.bfloat16)
    value = proj[:, (QH + 1) * HD:].astype(jnp.bfloat16)
    block = math.gcd(L, 256)
    query_blocks = query.reshape(L // block, block, QH, HD)
    pos_blocks = positions.reshape(L // block, block)

    def attend(pair):
        qblock, qpos = pair
        scores = jnp.einsum('bhd,kd->bhk', qblock.astype(jnp.float32), key.astype(jnp.float32))
        mask = positions[None, None, :] <= qpos[:, None, None]
        scores = jnp.where(mask, scores, -1e30)
        top = jnp.max(scores, axis=-1, keepdims=True)
        probs = jnp.where(mask, jnp.exp(scores - top), 0.0)
        total = jnp.sum(probs, axis=-1)
        rounded = probs.astype(jnp.bfloat16)
        mixed = jnp.einsum('bhk,kd->bhd', rounded.astype(jnp.float32), value.astype(jnp.float32))
        return (mixed / total[..., None]).astype(jnp.bfloat16).reshape(block, QH * HD)

    out = lax.map(attend, (query_blocks, pos_blocks))
    return out.reshape(L, QH * HD)


def reference(tokens, qkv_weight, span_pos):
    rows = jnp.arange(L, dtype=jnp.int32)
    positions = span_pos[rows // CH] * CH + rows % CH
    outs = [one_document(tokens[d], qkv_weight, positions) for d in range(DOCS)]
    return jnp.stack(outs, axis=0)
```

```python
import functools
import jax
import jax.numpy as jnp
from jax import lax
from jax.experimental import pallas as pl
from jax.experimental.pallas import tpu as pltpu
from jax.sharding import PartitionSpec as P

HD = 128
QH = 4
MESH = pl.DeviceIdType.MESH
F32 = jnp.float32
BF16 = jnp.bfloat16


def place():
    doc = lax.axis_index("doc")
    outer = lax.axis_index("outer")
    inner = lax.axis_index("inner")
    return inner // 2, doc * 2 + outer % 2, outer // 2, inner % 2


def device(x, y, z, c):
    x = lax.rem(x + 4, 4)
    y = lax.rem(y + 4, 4)
    z = lax.rem(z + 8, 8)
    return {"doc": y // 2, "outer": z * 2 + lax.rem(y, 2), "inner": x * 2 + c}


def nth(t):
    return ((t + 1) // 2) * (lax.rem(t, 2) * 2 - 1)


def rcopy(src, dst, ssem, rsem, dev):
    return pltpu.make_async_remote_copy(
        src_ref=src, dst_ref=dst, send_sem=ssem, recv_sem=rsem, device_id=dev, device_id_type=MESH
    )


def proj_kernel(
    tok, wsh, cos_ref, sin_ref, span, out,
    X, W, acc, rsib, sbf, rbf, QB, KV, S0, S1, P0, P1, o_acc, m_acc, l_acc, qpos, o_out, o_in, st_out, st_in,
    x_loc, x_s, x_r, w_loc, p_s, p_r, z_s, z_r, y_s, y_r, d_s, d_r, f_s, f_r,
    q_s, q_r, l_s, l_r, c_s, c_r, v_s, v_r, o_s, o_r,
):
    x, y, z, c = place()
    p = lax.rem(x, 2)
    src = lax.rem(y, 2) == p
    sgn = jnp.where(src, -1, 1)
    doc = y // 2
    d0 = jnp.where(src, doc, lax.rem(y + 3, 4) // 2)
    d1 = jnp.where(src, doc, lax.rem(y + 1, 4) // 2)
    ds = (d0, d1)
    rows = 128

    def wslot(zz, d, h):
        return W.at[zz * 2 + d, pl.ds(h * 192, 192), :]

    own = pltpu.make_async_copy(wsh.at[pl.ds(c * 384, 384), :], W.at[z * 2 + doc], w_loc)

    @pl.when(src)
    def _():
        own.start()

    def loc(zz):
        col = pl.multiple_of((zz * 2 + p) * 768 + c * 384, 128)
        return pltpu.make_async_copy(
            tok.at[0, :, pl.ds(col, 384)], X.at[zz, pl.ds(0, rows), :], x_loc.at[zz]
        )

    def start_loc(t, _):
        loc(lax.rem(z + nth(t) + 8, 8)).start()
        return 0

    lax.fori_loop(0, 8, start_loc, 0)

    barrier = pltpu.get_barrier_semaphore()
    peers = [device(x, y, z + 1, c), device(x, y, z - 1, c), device(x, y + 1, z, c), device(x, y - 1, z, c),
             device(x, y, z, 1 - c)]
    for a in (-1, 1):
        for e in (0, 1):
            peers.append(device(x + a, y, z, e))
    peers += [device(x, y, z + 2, c), device(x, y, z - 2, c),
              device(x + 1 - 2 * p, y + 1 - 2 * lax.rem(y, 2), z, c)]
    for dev in peers:
        pl.semaphore_signal(barrier, inc=1, device_id=dev, device_id_type=MESH)
    pl.semaphore_wait(barrier, len(peers))

    def p1(h):
        return rcopy(wslot(z, ds[h], h), wslot(z, ds[h], h), p_s.at[h], p_r.at[h],
                     device(x, y + (1 if h == 0 else -1), z, c))

    def ring(sign, h, k):
        zz = lax.rem(z - sign * (k - 1) + 16, 8)
        j = 0 if sign > 0 else 1
        return rcopy(wslot(zz, ds[h], h), wslot(zz, ds[h], h), z_s.at[j, h, k - 1], z_r.at[j, h, k - 1],
                     device(x, y, z + sign, c))

    def ring_in(sign, h, k):
        zz = lax.rem(z - sign * k + 16, 8)
        j = 0 if sign > 0 else 1
        return rcopy(wslot(zz, ds[h], h), wslot(zz, ds[h], h), z_s.at[j, h, k - 1], z_r.at[j, h, k - 1],
                     device(x, y, z + sign, c))

    def hops(sign, h):
        return 4 if (sign > 0) == (h == 0) else 3

    def yout(h, zz):
        return rcopy(wslot(zz, ds[h], h), wslot(zz, ds[h], h), y_s.at[h, zz], y_r.at[h, zz],
                     device(x, y + (sgn if h == 0 else -sgn), z, c))

    def yin(h, zz):
        return rcopy(wslot(zz, 1 - ds[h], h), wslot(zz, 1 - ds[h], h), y_s.at[h, zz], y_r.at[h, zz],
                     device(x, y + (sgn if h == 0 else -sgn), z, c))

    @pl.when(src)
    def _():
        own.wait()
        for h in (0, 1):
            p1(h).start()

    def xout(zz, j):
        pe = lax.rem(zz, 2)
        if j == 0:
            col = pl.multiple_of((zz * 2 + p) * 768 + (1 - c) * 384, 128)
            return rcopy(tok.at[0, :, pl.ds(col, 384)], X.at[zz, pl.ds(rows, rows), :],
                         x_s.at[zz, 0], x_r.at[zz, 0], device(x, y, z, 1 - c))
        px = x + jnp.where(p == pe, 1, -1)
        e = j - 1
        col = pl.multiple_of((zz * 2 + 1 - p) * 768 + e * 384, 128)
        return rcopy(tok.at[0, :, pl.ds(col, 384)], X.at[zz, pl.ds((2 + c) * rows, rows), :],
                     x_s.at[zz, j], x_r.at[zz, 1 + c], device(px, y, z, e))

    def xin(zz, j):
        pe = lax.rem(zz, 2)
        px = x + jnp.where(p == pe, 1, -1)
        dst = X.at[zz, pl.ds((1 + j) * rows, rows), :]
        return rcopy(dst, dst, x_s.at[zz, j], x_r.at[zz, j], device(px, y, z, c))

    def start_x(t, _):
        zz = lax.rem(z + nth(t) + 8, 8)
        for j in range(3):
            xout(zz, j).start()
        return 0

    @pl.when(src)
    def _():
        for h in (0, 1):
            for s in (1, -1):
                ring(s, h, 1).start()
            yout(h, z).start()

    lax.fori_loop(0, 8, start_x, 0)

    @pl.when(jnp.logical_not(src))
    def _():
        for h in (0, 1):
            p1(h).wait_recv()
            for s in (1, -1):
                ring(s, h, 1).start()
            yout(h, z).start()

    acc[...] = jnp.zeros_like(acc)

    def mm(zz):
        for h in (0, 1):
            yin(h, zz).wait_recv()
        loc(zz).wait()
        for j in range(3):
            xin(zz, j).wait_recv()
        pe = lax.rem(zz, 2)
        for d in (0, 1):
            r = jnp.dot(X[zz], W[zz * 2 + d], preferred_element_type=F32)
            acc[pl.ds(0, 256), pl.ds(d * 384, 384)] += r[:256]
            acc[pl.ds(pl.multiple_of(256 + pe * 256, 256), 256), pl.ds(d * 384, 384)] += r[256:]

    for k in range(1, 5):
        for h in (0, 1):
            for s in (1, -1):
                if k <= hops(s, h):
                    ring_in(s, h, k).wait_recv()
                    if k < hops(s, h):
                        ring(s, h, k + 1).start()
                    yout(h, lax.rem(z - s * k + 16, 8)).start()
        if k == 2:
            mm(z)
        if k >= 3:
            @functools.partial(lax.fori_loop, 0, 2, init_val=0)
            def _(t, _):
                mm(lax.rem(z + (k - 2) * (1 - 2 * t) + 8, 8))
                return 0

    @functools.partial(lax.fori_loop, 0, 3, init_val=0)
    def _(t, _):
        mm(lax.rem(z + nth(t + 5) + 8, 8))
        return 0

    parts = (pl.ds(512, 256), pl.ds(0, 512))

    def d2d(j, part):
        if j == 0:
            blk = 128
        else:
            blk = pl.multiple_of(256 * j + (1 - c) * 128, 128)
        return rcopy(acc.at[pl.ds(blk, 128), parts[part]], rsib.at[j, :, parts[part]],
                     d_s.at[part, j], d_r.at[part, j], device(x, y, z, 1 - c))

    def fin(pe, part):
        px = x + jnp.where(p == pe, 1, -1)
        return rcopy(sbf.at[pe, :, parts[part]], rbf.at[pe, :, parts[part]],
                     f_s.at[part, pe], f_r.at[part, pe], device(px, y, z, c))

    for part in (0, 1):
        for j in (1, 2, 0):
            d2d(j, part).start()
    for part in (0, 1):
        for pe in (0, 1):
            d2d(pe + 1, part).wait_recv()
            mine = acc[pl.ds(pl.multiple_of(256 + pe * 256 + c * 128, 128), 128), parts[part]]
            sbf[pe, :, parts[part]] = mine + rsib[pe + 1, :, parts[part]]
            fin(pe, part).start()

    def finish(part):
        d2d(0, part).wait_recv()
        total = acc[pl.ds(0, 128), parts[part]] + rsib[0, :, parts[part]]
        for pe in (0, 1):
            fin(pe, part).wait_recv()
            total = total + rbf[pe, :, parts[part]]
        return total

    def rot(v):
        return v * cos_ref[...] + pltpu.roll(v, 64, 1) * sin_ref[...]

    kv = finish(0)
    KV[z, c, 0, 0] = rot(kv[:, :HD]).astype(BF16)
    KV[z, c, 0, 1] = kv[:, HD:].T.astype(BF16)

    ylo = lax.rem(y, 2)
    xodd = lax.rem(x, 2)
    xk = lax.rem(x + 3 + 2 * xodd, 4)
    s4 = 1 - 2 * c
    sib = device(x, y, z, 1 - c)

    def ring8(v):
        return lax.rem(v + 16, 8)

    def mate(g):
        return device(x + lax.rem(g, 2) * (1 - 2 * xodd), y + (g // 2) * (1 - 2 * ylo), z, c)

    def qcopy(g):
        return rcopy(QB.at[0], QB.at[g], q_s.at[g - 1], q_r.at[g - 1], mate(g))

    def line(i, k, incoming=False):
        s = (1 - 2 * i) if k < 4 else s4
        hop = (0, 1, 2, 1, 2)[k]
        zz = ring8(z - s * (k if incoming else k - hop))
        ref = KV.at[zz, c, 0]
        return rcopy(ref, ref, l_s.at[i, k - 1], l_r.at[i, k - 1], device(x, y, z + s * hop, c))

    def cross(zz, incoming=False):
        return rcopy(KV.at[zz, c, 0], KV.at[zz, c, 1], c_s.at[zz], c_r.at[zz], device(xk, y, z, c))

    def over(zz, n, incoming=False):
        ref = KV.at[zz, 1 - c if incoming else c, n]
        return rcopy(ref, ref, v_s.at[zz, n], v_r.at[zz, n], sib)

    def arrived(i, k):
        line(i, k, True).wait_recv()
        zz = ring8(z - ((1 - 2 * i) if k < 4 else s4) * k)
        cross(zz).start()
        over(zz, 0).start()

    def crossed(zz):
        cross(zz).wait_recv()
        over(zz, 1).start()

    for k in (1, 2):
        for i in (0, 1):
            line(i, k).start()
        if k == 1:
            cross(z).start()
            over(z, 0).start()
    for i in (0, 1):
        arrived(i, 1)

    query = finish(1)
    for h in range(QH):
        q = (rot(query[:, h * HD:(h + 1) * HD]) * HD ** (-0.5)).astype(BF16)
        QB[0, :, h * 128:(h + 1) * 128] = q.T
    for g in (1, 2, 3):
        qcopy(g).start()
    for i in (0, 1):
        arrived(i, 2)
    for i in (0, 1):
        line(i, 3).start()
    line(0, 4).start()
    crossed(z)
    for k in (1, -1):
        crossed(ring8(z + k))

    lane = lax.broadcasted_iota(jnp.int32, (1, 512), 1)
    half = lax.rem(lane, 128) // 64
    NEG = -1e30
    for g in range(4):
        gx = x + (g % 2) * (1 - 2 * xodd)
        gy = ylo + (g // 2) * (1 - 2 * ylo)
        blk = ((z * 2 + gy) * 8 + gx * 2 + c) * 2
        qpos[g] = jnp.where(half == 0, span[blk], span[blk + 1])

    def row_mask():
        r = lax.broadcasted_iota(jnp.int32, (128, 512), 0)
        l = lax.rem(lax.broadcasted_iota(jnp.int32, (128, 512), 1), 128)
        return jnp.logical_and(r // 64 == l // 64, r <= l)

    def scores(zz, g, S):
        S[...] = jnp.dot(KV[zz, :, :, 0].reshape(512, 128), QB[g], preferred_element_type=F32)

    def soften(zz, g, S, Pb):
        qp = qpos[g]

        def kpos(b):
            xx = x if b // 2 % 2 == 0 else xk
            return span[((zz * 2 + ylo) * 8 + xx * 2 + b // 4) * 2 + b % 2]
        mx = None
        for b in range(8):
            t = jnp.max(S[b * 64:(b + 1) * 64, :].reshape(8, 8, 512), axis=0)
            t = jnp.where(kpos(b) < qp, t, NEG)
            mx = t if mx is None else jnp.maximum(mx, t)
        old = m_acc[g]
        new = jnp.maximum(old, jnp.max(mx, axis=0, keepdims=True))
        scale = jnp.exp(old - new)
        ls = None
        for b in range(8):
            lim = jnp.where(kpos(b) < qp, new, -NEG)
            pb = jnp.exp(S[b * 64:(b + 1) * 64, :] - lim)
            t = jnp.sum(pb.reshape(8, 8, 512), axis=0)
            ls = t if ls is None else ls + t
            Pb[b * 64:(b + 1) * 64, :] = pb.astype(BF16)
        vv = jnp.concatenate([KV[zz, e, n, 1] for e in range(2) for n in range(2)], axis=1)
        m_acc[g] = new
        l_acc[g] = l_acc[g] * scale + jnp.sum(ls, axis=0, keepdims=True)
        o_acc[g] = o_acc[g] * scale + jnp.dot(vv, Pb[...], preferred_element_type=F32)

    def ready(zz):
        for n in (0, 1):
            over(zz, n, True).wait_recv()

    sc = jnp.where(row_mask(), jnp.dot(KV[z, c, 0, 0], QB[0], preferred_element_type=F32), NEG)
    top = jnp.max(sc, axis=0, keepdims=True)
    pr = jnp.where(row_mask(), jnp.exp(sc - top), 0.0)
    m_acc[0] = top
    l_acc[0] = jnp.sum(pr, axis=0, keepdims=True)
    o_acc[0] = jnp.dot(KV[z, c, 0, 1], pr.astype(BF16), preferred_element_type=F32)
    for g in (1, 2, 3):
        m_acc[g] = jnp.full((1, 512), NEG, F32)
        l_acc[g] = jnp.zeros((1, 512), F32)
        o_acc[g] = jnp.zeros((128, 512), F32)
    for g in (1, 2, 3):
        qcopy(g).wait_recv()

    @functools.partial(lax.fori_loop, 0, 5, init_val=0)
    def _(t, _):
        @pl.when(t == 2)
        def _():
            for i in (0, 1):
                arrived(i, 3)
            arrived(0, 4)

        @pl.when(t == 3)
        def _():
            for k in (2, -2):
                crossed(ring8(z + k))
        zz = ring8(z + nth(t))
        ready(zz)
        scores(zz, 3, S0)
        scores(zz, 2, S1)
        soften(zz, 3, S0, P0)
        scores(zz, 1, S0)
        soften(zz, 2, S1, P1)
        scores(zz, 0, S1)
        soften(zz, 1, S0, P0)
        soften(zz, 0, S1, P1)
        return 0

    tail = [ring8(z + k) for k in (3, -3, 4)]
    for zz in tail:
        crossed(zz)
    for zz in tail:
        ready(zz)

    def ocopy(g):
        return rcopy(o_out.at[g - 1], o_in.at[g - 1], o_s.at[0, g - 1], o_r.at[0, g - 1], mate(g))

    def stcopy(g):
        return rcopy(st_out.at[g - 1], st_in.at[g - 1], o_s.at[1, g - 1], o_r.at[1, g - 1], mate(g))

    @functools.partial(lax.fori_loop, 0, 4, init_val=0)
    def _(t, _):
        g = 3 - t
        scores(tail[0], g, S0)
        scores(tail[1], g, S1)
        soften(tail[0], g, S0, P0)
        scores(tail[2], g, S0)
        soften(tail[1], g, S1, P1)
        soften(tail[2], g, S0, P0)

        @pl.when(g > 0)
        def _():
            l2 = l_acc[g]
            o_out[g - 1] = (o_acc[g] * jnp.where(l2 > 0.0, 1.0 / l2, 0.0)).astype(BF16)
            st_out[g - 1, 0:1, :] = m_acc[g]
            st_out[g - 1, 1:2, :] = l2
            ocopy(g).start()
            stcopy(g).start()
        return 0

    for g in (3, 2, 1):
        stcopy(g).wait_recv()
        ocopy(g).wait_recv()
    mm_ = m_acc[0]
    for g in range(3):
        mm_ = jnp.maximum(mm_, st_in[g, 0:1, :])
    e1 = jnp.exp(m_acc[0] - mm_)
    ws = [st_in[g, 1:2, :] * jnp.exp(st_in[g, 0:1, :] - mm_) for g in range(3)]
    inv = 1.0 / (l_acc[0] * e1 + ws[0] + ws[1] + ws[2])
    res = o_acc[0] * (e1 * inv)
    for g in range(3):
        res = res + o_in[g].astype(F32) * (ws[g] * inv)
    for h in range(QH):
        out[0, :, h * 128:(h + 1) * 128] = res[:, h * 128:(h + 1) * 128].T.astype(BF16)

    @pl.when(src)
    def _():
        for h in (0, 1):
            p1(h).wait_send()
    for h in (0, 1):
        for s in (1, -1):
            for k in range(1, hops(s, h) + 1):
                ring(s, h, k).wait_send()

    @functools.partial(lax.fori_loop, 0, 8, init_val=0)
    def _(t, _):
        for h in (0, 1):
            yout(h, t).wait_send()
        for j in range(3):
            xout(t, j).wait_send()
        return 0

    for part in (0, 1):
        for j in range(3):
            d2d(j, part).wait_send()
        for pe in (0, 1):
            fin(pe, part).wait_send()
    for g in (1, 2, 3):
        qcopy(g).wait_send()
        ocopy(g).wait_send()
        stcopy(g).wait_send()
    for k in range(1, 5):
        for i in (0, 1):
            if k < 4 or i == 0:
                line(i, k).wait_send()

    @functools.partial(lax.fori_loop, 0, 8, init_val=0)
    def _(t, _):
        cross(t).wait_send()
        for n in (0, 1):
            over(t, n).wait_send()
        return 0


def sublayer(tokens, wsh, cosine, sine, span):
    dma = pltpu.SemaphoreType.DMA
    vm = pl.BlockSpec(memory_space=pltpu.VMEM)
    return pl.pallas_call(
        proj_kernel,
        out_shape=jax.ShapeDtypeStruct((1, 128, 512), BF16),
        in_specs=[pl.BlockSpec(memory_space=pl.ANY)] * 2 + [vm] * 2 + [pl.BlockSpec(memory_space=pltpu.SMEM)],
        out_specs=vm,
        scratch_shapes=[
            pltpu.VMEM((8, 512, 384), BF16),
            pltpu.VMEM((16, 384, 384), BF16),
            pltpu.VMEM((768, 768), F32),
            pltpu.VMEM((3, 128, 768), F32),
            pltpu.VMEM((2, 128, 768), F32),
            pltpu.VMEM((2, 128, 768), F32),
            pltpu.VMEM((4, 128, 512), BF16),
            pltpu.VMEM((8, 2, 2, 2, 128, 128), BF16),
            pltpu.VMEM((512, 512), F32),
            pltpu.VMEM((512, 512), F32),
            pltpu.VMEM((512, 512), BF16),
            pltpu.VMEM((512, 512), BF16),
            pltpu.VMEM((4, 128, 512), F32),
            pltpu.VMEM((4, 1, 512), F32),
            pltpu.VMEM((4, 1, 512), F32),
            pltpu.VMEM((4, 1, 512), jnp.int32),
            pltpu.VMEM((3, 128, 512), BF16),
            pltpu.VMEM((3, 128, 512), BF16),
            pltpu.VMEM((3, 8, 512), F32),
            pltpu.VMEM((3, 8, 512), F32),
            dma((8,)), dma((8, 3)), dma((8, 3)), dma,
            dma((2,)), dma((2,)), dma((2, 2, 4)), dma((2, 2, 4)), dma((2, 8)), dma((2, 8)),
            dma((2, 3)), dma((2, 3)), dma((2, 2)), dma((2, 2)),
            dma((3,)), dma((3,)), dma((2, 4)), dma((2, 4)), dma((8,)), dma((8,)),
            dma((8, 2)), dma((8, 2)), dma((2, 3)), dma((2, 3)),
        ],
        compiler_params=pltpu.CompilerParams(
            collective_id=0, has_side_effects=True, vmem_limit_bytes=56 * 2**20
        ),
    )(tokens, wsh, cosine, sine, span)


def rope(blocks):
    freq = 1000000.0 ** (-jnp.arange(64, dtype=F32) * 2.0 / HD)
    positions = (blocks[:, None] * 64 + jnp.arange(64, dtype=jnp.int32)[None, :]).reshape(-1)
    angle = positions.astype(F32)[:, None] * freq[None, :]
    c, s = jnp.cos(angle), jnp.sin(angle)
    return jnp.concatenate([c, c], axis=1), jnp.concatenate([-s, s], axis=1)


def per_device(tokens, qkv_weight, span_pos):
    seq = lax.axis_index("outer") * 8 + lax.axis_index("inner")
    blocks = lax.dynamic_slice(span_pos, (seq * 2,), (2,))
    cosine, sine = rope(blocks)
    return sublayer(tokens, qkv_weight, cosine, sine, span_pos)


def solution(mesh):
    in_specs = (P("doc", ("outer", "inner"), None), P("outer", "doc"), P())
    out_specs = P("doc", ("outer", "inner"), None)
    return jax.shard_map(
        per_device, mesh=mesh, in_specs=in_specs, out_specs=out_specs, check_vma=False
    )
```

```python
import functools
import jax
import jax.numpy as jnp
from jax import lax
from jax.experimental import pallas as pl
from jax.experimental.pallas import tpu as pltpu
from jax.sharding import PartitionSpec as P

HD = 128
QH = 4
MESH = pl.DeviceIdType.MESH
F32 = jnp.float32
BF16 = jnp.bfloat16


def place():
    doc = lax.axis_index("doc")
    outer = lax.axis_index("outer")
    inner = lax.axis_index("inner")
    return inner // 2, doc * 2 + outer % 2, outer // 2, inner % 2


def device(x, y, z, c):
    x = lax.rem(x + 4, 4)
    y = lax.rem(y + 4, 4)
    z = lax.rem(z + 8, 8)
    return {"doc": y // 2, "outer": z * 2 + lax.rem(y, 2), "inner": x * 2 + c}


def nth(t):
    return ((t + 1) // 2) * (lax.rem(t, 2) * 2 - 1)


def rcopy(src, dst, ssem, rsem, dev):
    return pltpu.make_async_remote_copy(
        src_ref=src, dst_ref=dst, send_sem=ssem, recv_sem=rsem, device_id=dev, device_id_type=MESH
    )


def sublayer_kernel(
    tok, wsh, freq, span, out,
    X, W1, W2, acc, rsib, psend, precv, QB, KV, cos_ref, sin_ref, S0, S1, P0, P1,
    o_acc, m_acc, l_acc, qpos, o_out, o_in, st_out, st_in,
    x_loc, x_s, x_r, w_loc, p_s, p_r, z_s, z_r, y_s, y_r, d_s, d_r, f_s, f_r,
    q_s, q_r, l_s, l_r, c_s, c_r, v_s, v_r, o_s, o_r,
):
    x, y, z, c = place()
    p = lax.rem(x, 2)
    ylo = lax.rem(y, 2)
    src = ylo == p
    sgn = jnp.where(src, -1, 1)
    doc = y // 2
    d0 = jnp.where(src, doc, lax.rem(y + 3, 4) // 2)
    d1 = jnp.where(src, doc, lax.rem(y + 1, 4) // 2)
    ds = (d0, d1)
    rows = 128
    xk = lax.rem(x + 3 + 2 * p, 4)
    s4 = 1 - 2 * c
    sib = device(x, y, z, 1 - c)
    NEG = -1e30

    def ring8(v):
        return lax.rem(v + 16, 8)

    def slot(zz, d, h, n):
        if n < 2:
            return W1.at[zz * 2 + d, pl.ds(h * 192 + n * 96, 96), :]
        return W2.at[zz * 2 + d, pl.ds(h * 192, 192), :]

    def own(n):
        if n == 0:
            col = pl.multiple_of(doc * 128, 128)
            return pltpu.make_async_copy(
                wsh.at[pl.ds(c * 384, 384), pl.ds(col, 256)], W1.at[z * 2 + doc], w_loc.at[0])
        col = pl.multiple_of((1 - doc) * 256, 128)
        return pltpu.make_async_copy(
            wsh.at[pl.ds(c * 384, 384), pl.ds(col, 128)], W2.at[z * 2 + doc], w_loc.at[1])

    @pl.when(src)
    def _():
        own(0).start()
        own(1).start()

    def loc(zz):
        col = pl.multiple_of((zz * 2 + p) * 768 + c * 384, 128)
        return pltpu.make_async_copy(
            tok.at[0, :, pl.ds(col, 384)], X.at[zz, pl.ds(0, rows), :], x_loc.at[zz]
        )

    def start_loc(t, _):
        loc(ring8(z + nth(t))).start()
        return 0

    lax.fori_loop(0, 8, start_loc, 0)

    barrier = pltpu.get_barrier_semaphore()
    peers = [device(x, y, z + 1, c), device(x, y, z - 1, c), device(x, y + 1, z, c), device(x, y - 1, z, c), sib]
    for a in (-1, 1):
        for e in (0, 1):
            peers.append(device(x + a, y, z, e))
    peers += [device(x, y, z + 2, c), device(x, y, z - 2, c), device(x + 1 - 2 * p, y + 1 - 2 * ylo, z, c)]
    for dev in peers:
        pl.semaphore_signal(barrier, inc=1, device_id=dev, device_id_type=MESH)
    pl.semaphore_wait(barrier, len(peers))

    def p1(h, n):
        ref = slot(z, ds[h], h, n)
        return rcopy(ref, ref, p_s.at[h, n], p_r.at[h, n], device(x, y + (1 if h == 0 else -1), z, c))

    def ring(sign, h, k, n, incoming=False):
        zz = ring8(z - sign * (k if incoming else k - 1))
        j = 0 if sign > 0 else 1
        ref = slot(zz, ds[h], h, n)
        return rcopy(ref, ref, z_s.at[j, h, k - 1, n], z_r.at[j, h, k - 1, n], device(x, y, z + sign, c))

    def hops(sign, h):
        return 4 if (sign > 0) == (h == 0) else 3

    def yout(h, zz, n):
        ref = slot(zz, ds[h], h, n)
        return rcopy(ref, ref, y_s.at[h, zz, n], y_r.at[h, zz, n],
                     device(x, y + (sgn if h == 0 else -sgn), z, c))

    def yin(h, zz, n):
        ref = slot(zz, 1 - ds[h], h, n)
        return rcopy(ref, ref, y_s.at[h, zz, n], y_r.at[h, zz, n],
                     device(x, y + (sgn if h == 0 else -sgn), z, c))

    def xout(zz, j):
        pe = lax.rem(zz, 2)
        if j == 0:
            col = pl.multiple_of((zz * 2 + p) * 768 + (1 - c) * 384, 128)
            return rcopy(tok.at[0, :, pl.ds(col, 384)], X.at[zz, pl.ds(rows, rows), :],
                         x_s.at[zz, 0], x_r.at[zz, 0], sib)
        px = x + jnp.where(p == pe, 1, -1)
        e = j - 1
        col = pl.multiple_of((zz * 2 + 1 - p) * 768 + e * 384, 128)
        return rcopy(tok.at[0, :, pl.ds(col, 384)], X.at[zz, pl.ds((2 + c) * rows, rows), :],
                     x_s.at[zz, j], x_r.at[zz, 1 + c], device(px, y, z, e))

    def xin(zz, j):
        px = x + jnp.where(p == lax.rem(zz, 2), 1, -1)
        dst = X.at[zz, pl.ds((1 + j) * rows, rows), :]
        return rcopy(dst, dst, x_s.at[zz, j], x_r.at[zz, j], device(px, y, z, c))

    def start_x(t, _):
        zz = ring8(z + nth(t))
        for j in range(3):
            xout(zz, j).start()
        return 0

    def spread(h, n):
        for s in (1, -1):
            ring(s, h, 1, n).start()
        yout(h, z, n).start()

    def feed(ns):
        @pl.when(src)
        def _():
            for n in ns:
                for h in (0, 1):
                    p1(h, n).start()
            for n in ns:
                for h in (0, 1):
                    spread(h, n)

    def enter(ns):
        @pl.when(jnp.logical_not(src))
        def _():
            for n in ns:
                for h in (0, 1):
                    p1(h, n).wait_recv()
                    spread(h, n)

    def hop(k, ns):
        for n in ns:
            for h in (0, 1):
                for s in (1, -1):
                    if k <= hops(s, h):
                        ring(s, h, k, n, True).wait_recv()
                        if k < hops(s, h):
                            ring(s, h, k + 1, n).start()
                        yout(h, ring8(z - s * k), n).start()

    @pl.when(src)
    def _():
        own(0).wait()
        own(1).wait()

    feed((0, 1))
    lax.fori_loop(0, 8, start_x, 0)
    enter((0, 1))

    acc[...] = jnp.zeros_like(acc)
    row = lax.broadcasted_iota(jnp.int32, (128, 128), 0)
    blk0 = ((z * 2 + ylo) * 8 + x * 2 + c) * 2
    pos = jnp.where(row < 64, span[blk0], span[blk0 + 1]) * 64 + lax.rem(row, 64)
    angle = pos.astype(F32) * freq[...]
    cos_ref[...] = jnp.cos(angle)
    sin_ref[...] = jnp.where(lax.broadcasted_iota(jnp.int32, (128, 128), 1) < 64, -1.0, 1.0) * jnp.sin(angle)

    def add(part, zz, w):
        r = jnp.dot(X[zz], w, preferred_element_type=F32)
        acc[part, pl.ds(0, 256), :] += r[:256]
        acc[part, pl.ds(pl.multiple_of(256 + lax.rem(zz, 2) * 256, 256), 256), :] += r[256:]

    def mm1(zz):
        for n in (0, 1):
            for h in (0, 1):
                yin(h, zz, n).wait_recv()
        loc(zz).wait()
        for j in range(3):
            xin(zz, j).wait_recv()
        for d in (0, 1):
            add(1 - d, zz, W1[zz * 2 + d])

    def mm2(zz):
        for h in (0, 1):
            yin(h, zz, 2).wait_recv()
        add(2, zz, jnp.concatenate([W2[zz * 2], W2[zz * 2 + 1]], axis=1))

    def each(f, lo, hi):
        @functools.partial(lax.fori_loop, lo, hi, init_val=0)
        def _(t, _):
            f(ring8(z + nth(t)))
            return 0

    def d2d(j, part):
        blk = 128 if j == 0 else pl.multiple_of(256 * j + (1 - c) * 128, 128)
        return rcopy(acc.at[part, pl.ds(blk, 128), :], rsib.at[part, j], d_s.at[part, j], d_r.at[part, j], sib)

    def fin(pe, part):
        px = x + jnp.where(p == pe, 1, -1)
        return rcopy(psend.at[part, pe], precv.at[part, pe], f_s.at[part, pe], f_r.at[part, pe],
                     device(px, y, z, c))

    def to_sibling(part):
        for j in (1, 2, 0):
            d2d(j, part).start()

    def to_chips(part):
        for pe in (0, 1):
            d2d(pe + 1, part).wait_recv()
            mine = acc[part, pl.ds(pl.multiple_of(256 + pe * 256 + c * 128, 128), 128), :]
            psend[part, pe] = mine + rsib[part, pe + 1]
            fin(pe, part).start()

    def finish(part):
        d2d(0, part).wait_recv()
        total = acc[part, pl.ds(0, 128), :] + rsib[part, 0]
        for pe in (0, 1):
            fin(pe, part).wait_recv()
            total = total + precv[part, pe]
        return total

    def rot(v):
        return v * cos_ref[...] + pltpu.roll(v, 64, 1) * sin_ref[...]

    def mate(g):
        return device(x + lax.rem(g, 2) * (1 - 2 * p), y + (g // 2) * (1 - 2 * ylo), z, c)

    def qcopy(g, pr):
        return rcopy(QB.at[pr, 0, :, pl.ds(0, 256)], QB.at[pr, g // 2, :, pl.ds((g % 2) * 256, 256)],
                     q_s.at[pr, g - 1], q_r.at[pr, g - 1], mate(g))

    def make_queries(pr):
        total = finish(1 + pr)
        for hh in (0, 1):
            q = (rot(total[:, hh * HD:(hh + 1) * HD]) * HD ** (-0.5)).astype(BF16)
            QB[pr, 0, :, hh * 128:(hh + 1) * 128] = q.T
        for g in (3, 2, 1):
            qcopy(g, pr).start()

    def line(i, k, incoming=False):
        s = (1 - 2 * i) if k < 4 else s4
        far = (0, 1, 2, 1, 2)[k]
        zz = ring8(z - s * (k if incoming else k - far))
        ref = KV.at[zz, c, 0]
        return rcopy(ref, ref, l_s.at[i, k - 1], l_r.at[i, k - 1], device(x, y, z + s * far, c))

    def cross(zz):
        return rcopy(KV.at[zz, c, 0], KV.at[zz, c, 1], c_s.at[zz], c_r.at[zz], device(xk, y, z, c))

    def over(zz, n, incoming=False):
        ref = KV.at[zz, 1 - c if incoming else c, n]
        return rcopy(ref, ref, v_s.at[zz, n], v_r.at[zz, n], sib)

    def arrived(i, k):
        line(i, k, True).wait_recv()
        zz = ring8(z - ((1 - 2 * i) if k < 4 else s4) * k)
        cross(zz).start()
        over(zz, 0).start()

    def crossed(zz):
        cross(zz).wait_recv()
        over(zz, 1).start()

    def scores(zz, B, S):
        S[...] = jnp.dot(KV[zz, :, :, 0].reshape(512, 128), QB[B // 2, lax.rem(B, 2)],
                         preferred_element_type=F32)

    def soften(zz, B, S, Pb):
        qp = qpos[lax.rem(B, 2)]

        def kpos(b):
            xx = x if b // 2 % 2 == 0 else xk
            return span[((zz * 2 + ylo) * 8 + xx * 2 + b // 4) * 2 + b % 2]
        mx = None
        for b in range(8):
            t = jnp.max(S[b * 64:(b + 1) * 64, :].reshape(8, 8, 512), axis=0)
            t = jnp.where(kpos(b) < qp, t, NEG)
            mx = t if mx is None else jnp.maximum(mx, t)
        old = m_acc[B]
        new = jnp.maximum(old, jnp.max(mx, axis=0, keepdims=True))
        scale = jnp.exp(old - new)
        ls = None
        for b in range(8):
            lim = jnp.where(kpos(b) < qp, new, -NEG)
            pb = jnp.exp(S[b * 64:(b + 1) * 64, :] - lim)
            t = jnp.sum(pb.reshape(8, 8, 512), axis=0)
            ls = t if ls is None else ls + t
            Pb[b * 64:(b + 1) * 64, :] = pb.astype(BF16)
        vv = jnp.concatenate([KV[zz, e, n, 1] for e in range(2) for n in range(2)], axis=1)
        m_acc[B] = new
        l_acc[B] = l_acc[B] * scale + jnp.sum(ls, axis=0, keepdims=True)
        o_acc[B] = o_acc[B] * scale + jnp.dot(vv, Pb[...], preferred_element_type=F32)

    def ready(zz):
        for n in (0, 1):
            over(zz, n, True).wait_recv()

    def prepare():
        lane = lax.broadcasted_iota(jnp.int32, (1, 512), 1)
        half = lax.rem(lane, 128) // 64
        for j in (0, 1):
            ps = []
            for g in (2 * j, 2 * j + 1):
                gx = x + (g % 2) * (1 - 2 * p)
                gy = ylo + (g // 2) * (1 - 2 * ylo)
                blk = ((z * 2 + gy) * 8 + gx * 2 + c) * 2
                ps.append(jnp.where(half == 0, span[blk], span[blk + 1]))
            qpos[j] = jnp.where(lane < 256, ps[0], ps[1])
        m_acc[...] = jnp.full((4, 1, 512), NEG, F32)
        l_acc[...] = jnp.zeros((4, 1, 512), F32)
        o_acc[...] = jnp.zeros((4, 128, 512), F32)

    def diagonal(pr):
        r = lax.broadcasted_iota(jnp.int32, (128, 256), 0)
        l = lax.rem(lax.broadcasted_iota(jnp.int32, (128, 256), 1), 128)
        ok = jnp.logical_and(r // 64 == l // 64, r <= l)
        sc = jnp.dot(KV[z, c, 0, 0], QB[pr, 0, :, 0:256], preferred_element_type=F32)
        sc = jnp.where(ok, sc, NEG)
        top = jnp.max(sc, axis=0, keepdims=True)
        pb = jnp.where(ok, jnp.exp(sc - top), 0.0)
        m_acc[2 * pr, :, 0:256] = top
        l_acc[2 * pr, :, 0:256] = jnp.sum(pb, axis=0, keepdims=True)
        o_acc[2 * pr, :, 0:256] = jnp.dot(KV[z, c, 0, 1], pb.astype(BF16), preferred_element_type=F32)

    def ocopy(g, pr):
        return rcopy(o_out.at[pr, g - 1], o_in.at[pr, g - 1], o_s.at[0, pr, g - 1], o_r.at[0, pr, g - 1], mate(g))

    def stcopy(g, pr):
        return rcopy(st_out.at[pr, g - 1], st_in.at[pr, g - 1], o_s.at[1, pr, g - 1], o_r.at[1, pr, g - 1], mate(g))

    def give(g, pr):
        B, lo = 2 * pr + g // 2, (g % 2) * 256
        l2 = l_acc[B, :, lo:lo + 256]
        o_out[pr, g - 1] = (o_acc[B, :, lo:lo + 256] * jnp.where(l2 > 0.0, 1.0 / l2, 0.0)).astype(BF16)
        st_out[pr, g - 1, 0:1, :] = m_acc[B, :, lo:lo + 256]
        st_out[pr, g - 1, 1:2, :] = l2
        ocopy(g, pr).start()
        stcopy(g, pr).start()

    def merge(pr):
        for g in (3, 2, 1):
            stcopy(g, pr).wait_recv()
            ocopy(g, pr).wait_recv()
        m0, l0 = m_acc[2 * pr, :, 0:256], l_acc[2 * pr, :, 0:256]
        top = m0
        for g in range(3):
            top = jnp.maximum(top, st_in[pr, g, 0:1, :])
        e0 = jnp.exp(m0 - top)
        ws = [st_in[pr, g, 1:2, :] * jnp.exp(st_in[pr, g, 0:1, :] - top) for g in range(3)]
        inv = 1.0 / (l0 * e0 + ws[0] + ws[1] + ws[2])
        res = o_acc[2 * pr, :, 0:256] * (e0 * inv)
        for g in range(3):
            res = res + o_in[pr, g].astype(F32) * (ws[g] * inv)
        for hh in (0, 1):
            h = 2 * pr + hh
            out[0, :, h * 128:(h + 1) * 128] = res[:, hh * 128:(hh + 1) * 128].T.astype(BF16)

    hop(1, (0, 1))
    hop(2, (0, 1))
    each(mm1, 0, 1)
    feed((2,))
    hop(3, (0, 1))
    each(mm1, 1, 3)
    enter((2,))
    hop(4, (0, 1))
    each(mm1, 3, 5)
    hop(1, (2,))
    each(mm1, 5, 8)
    to_sibling(0)
    to_sibling(1)
    hop(2, (2,))
    to_chips(0)
    to_chips(1)
    prepare()
    hop(3, (2,))

    kv = finish(0)
    KV[z, c, 0, 0] = rot(kv[:, :HD]).astype(BF16)
    KV[z, c, 0, 1] = kv[:, HD:].T.astype(BF16)
    for k in (1, 2):
        for i in (0, 1):
            line(i, k).start()
        if k == 1:
            cross(z).start()
            over(z, 0).start()
    hop(4, (2,))
    each(mm2, 0, 5)
    make_queries(0)
    for i in (0, 1):
        arrived(i, 1)
    each(mm2, 5, 8)
    to_sibling(2)
    for i in (0, 1):
        arrived(i, 2)
    for i in (0, 1):
        line(i, 3).start()
    line(0, 4).start()
    to_chips(2)
    for k in (0, 1, -1):
        crossed(ring8(z + k))
    diagonal(0)
    for g in (3, 2, 1):
        qcopy(g, 0).wait_recv()

    @functools.partial(lax.fori_loop, 0, 8, init_val=0)
    def _(t, _):
        @pl.when(t == 1)
        def _():
            make_queries(1)

        @pl.when(t == 2)
        def _():
            for i in (0, 1):
                arrived(i, 3)
            arrived(0, 4)

        @pl.when(t == 3)
        def _():
            for k in (2, -2):
                crossed(ring8(z + k))

        @pl.when(t == 5)
        def _():
            for k in (3, -3, 4):
                crossed(ring8(z + k))
        zz = ring8(z + nth(t))
        ready(zz)
        scores(zz, 1, S0)
        scores(zz, 0, S1)
        soften(zz, 1, S0, P0)
        soften(zz, 0, S1, P1)
        return 0

    for g in (3, 2, 1):
        give(g, 0)
    diagonal(1)
    for g in (3, 2, 1):
        qcopy(g, 1).wait_recv()

    def sweep(B):
        scores(z, B, S0)

        @functools.partial(lax.fori_loop, 0, 4, init_val=0)
        def _(t, _):
            za, zb, zc = [ring8(z + nth(lax.rem(2 * t + n, 8))) for n in range(3)]
            scores(zb, B, S1)
            soften(za, B, S0, P0)
            scores(zc, B, S0)
            soften(zb, B, S1, P1)
            return 0

    sweep(3)
    give(3, 1)
    give(2, 1)
    sweep(2)
    give(1, 1)
    merge(0)
    merge(1)

    @pl.when(src)
    def _():
        for h in (0, 1):
            for n in range(3):
                p1(h, n).wait_send()
    for h in (0, 1):
        for s in (1, -1):
            for k in range(1, hops(s, h) + 1):
                for n in range(3):
                    ring(s, h, k, n).wait_send()
    for part in range(3):
        for j in range(3):
            d2d(j, part).wait_send()
        for pe in (0, 1):
            fin(pe, part).wait_send()
    for pr in (0, 1):
        for g in (1, 2, 3):
            qcopy(g, pr).wait_send()
            ocopy(g, pr).wait_send()
            stcopy(g, pr).wait_send()
    for k in range(1, 5):
        for i in (0, 1):
            if k < 4 or i == 0:
                line(i, k).wait_send()

    @functools.partial(lax.fori_loop, 0, 8, init_val=0)
    def _(t, _):
        for h in (0, 1):
            for n in range(3):
                yout(h, t, n).wait_send()
        for j in range(3):
            xout(t, j).wait_send()
        cross(t).wait_send()
        for n in (0, 1):
            over(t, n).wait_send()
        return 0


def sublayer(tokens, wsh, freq, span):
    dma = pltpu.SemaphoreType.DMA
    vm = pl.BlockSpec(memory_space=pltpu.VMEM)
    return pl.pallas_call(
        sublayer_kernel,
        out_shape=jax.ShapeDtypeStruct((1, 128, 512), BF16),
        in_specs=[pl.BlockSpec(memory_space=pl.ANY)] * 2 + [vm] + [pl.BlockSpec(memory_space=pltpu.SMEM)],
        out_specs=vm,
        scratch_shapes=[
            pltpu.VMEM((8, 512, 384), BF16),
            pltpu.VMEM((16, 384, 256), BF16),
            pltpu.VMEM((16, 384, 128), BF16),
            pltpu.VMEM((3, 768, 256), F32),
            pltpu.VMEM((3, 3, 128, 256), F32),
            pltpu.VMEM((3, 2, 128, 256), F32),
            pltpu.VMEM((3, 2, 128, 256), F32),
            pltpu.VMEM((2, 2, 128, 512), BF16),
            pltpu.VMEM((8, 2, 2, 2, 128, 128), BF16),
            pltpu.VMEM((128, 128), F32),
            pltpu.VMEM((128, 128), F32),
            pltpu.VMEM((512, 512), F32),
            pltpu.VMEM((512, 512), F32),
            pltpu.VMEM((512, 512), BF16),
            pltpu.VMEM((512, 512), BF16),
            pltpu.VMEM((4, 128, 512), F32),
            pltpu.VMEM((4, 1, 512), F32),
            pltpu.VMEM((4, 1, 512), F32),
            pltpu.VMEM((2, 1, 512), jnp.int32),
            pltpu.VMEM((2, 3, 128, 256), BF16),
            pltpu.VMEM((2, 3, 128, 256), BF16),
            pltpu.VMEM((2, 3, 8, 256), F32),
            pltpu.VMEM((2, 3, 8, 256), F32),
            dma((8,)), dma((8, 3)), dma((8, 3)), dma((2,)),
            dma((2, 3)), dma((2, 3)), dma((2, 2, 4, 3)), dma((2, 2, 4, 3)), dma((2, 8, 3)), dma((2, 8, 3)),
            dma((3, 3)), dma((3, 3)), dma((3, 2)), dma((3, 2)),
            dma((2, 3)), dma((2, 3)), dma((2, 4)), dma((2, 4)), dma((8,)), dma((8,)),
            dma((8, 2)), dma((8, 2)), dma((2, 2, 3)), dma((2, 2, 3)),
        ],
        compiler_params=pltpu.CompilerParams(
            collective_id=0, has_side_effects=True, vmem_limit_bytes=56 * 2**20
        ),
    )(tokens, wsh, freq, span)


def per_device(tokens, qkv_weight, span_pos):
    freq = 1000000.0 ** (-jnp.arange(64, dtype=F32) * 2.0 / HD)
    freq = jnp.concatenate([freq, freq])[None, :]
    return sublayer(tokens, qkv_weight, freq, span_pos)


def solution(mesh):
    in_specs = (P("doc", ("outer", "inner"), None), P("outer", "doc"), P())
    out_specs = P("doc", ("outer", "inner"), None)
    return jax.shard_map(
        per_device, mesh=mesh, in_specs=in_specs, out_specs=out_specs, check_vma=False
    )
```

```python
import functools
import jax
import jax.numpy as jnp
from jax import lax
from jax.experimental import pallas as pl
from jax.experimental.pallas import tpu as pltpu
from jax.sharding import PartitionSpec as P

HD = 128
QH = 4
MESH = pl.DeviceIdType.MESH
F32 = jnp.float32
BF16 = jnp.bfloat16


def place():
    doc = lax.axis_index("doc")
    outer = lax.axis_index("outer")
    inner = lax.axis_index("inner")
    return inner // 2, doc * 2 + outer % 2, outer // 2, inner % 2


def device(x, y, z, c):
    x = lax.rem(x + 4, 4)
    y = lax.rem(y + 4, 4)
    z = lax.rem(z + 8, 8)
    return {"doc": y // 2, "outer": z * 2 + lax.rem(y, 2), "inner": x * 2 + c}


def nth(t):
    return ((t + 1) // 2) * (lax.rem(t, 2) * 2 - 1)


def rcopy(src, dst, ssem, rsem, dev):
    return pltpu.make_async_remote_copy(
        src_ref=src, dst_ref=dst, send_sem=ssem, recv_sem=rsem, device_id=dev, device_id_type=MESH
    )


def sublayer_kernel(
    tok, wsh, freq, span, out,
    X, W1, W2, acc, rsib, psend, precv, QB, KV, cos_ref, sin_ref, S0, S1, P0, P1,
    o_acc, m_acc, l_acc, qpos, o_out, o_in, st_out, st_in,
    x_loc, x_s, x_r, w_loc, p_s, p_r, z_s, z_r, y_s, y_r, d_s, d_r, f_s, f_r,
    q_s, q_r, l_s, l_r, n_s, n_r, c_s, c_r, v_s, v_r, o_s, o_r,
):
    x, y, z, c = place()
    p = lax.rem(x, 2)
    ylo = lax.rem(y, 2)
    src = ylo == p
    sgn = jnp.where(src, -1, 1)
    doc = y // 2
    d0 = jnp.where(src, doc, lax.rem(y + 3, 4) // 2)
    d1 = jnp.where(src, doc, lax.rem(y + 1, 4) // 2)
    ds = (d0, d1)
    rows = 128
    xk = lax.rem(x + 3 + 2 * p, 4)
    s4 = 1 - 2 * c
    sib = device(x, y, z, 1 - c)
    NEG = -1e30

    def ring8(v):
        return lax.rem(v + 16, 8)

    def slot(zz, d, h, n):
        if n < 2:
            return W1.at[zz * 2 + d, pl.ds(h * 192 + n * 96, 96), :]
        return W2.at[zz * 2 + d, pl.ds(h * 192, 192), :]

    def own(n):
        if n == 0:
            col = pl.multiple_of(doc * 128, 128)
            return pltpu.make_async_copy(
                wsh.at[pl.ds(c * 384, 384), pl.ds(col, 256)], W1.at[z * 2 + doc], w_loc.at[0])
        col = pl.multiple_of((1 - doc) * 256, 128)
        return pltpu.make_async_copy(
            wsh.at[pl.ds(c * 384, 384), pl.ds(col, 128)], W2.at[z * 2 + doc], w_loc.at[1])

    @pl.when(src)
    def _():
        own(0).start()
        own(1).start()

    def loc(zz):
        col = pl.multiple_of((zz * 2 + p) * 768 + c * 384, 128)
        return pltpu.make_async_copy(
            tok.at[0, :, pl.ds(col, 384)], X.at[zz, pl.ds(0, rows), :], x_loc.at[zz]
        )

    def start_loc(t, _):
        loc(ring8(z + nth(t))).start()
        return 0

    lax.fori_loop(0, 8, start_loc, 0)

    barrier = pltpu.get_barrier_semaphore()
    peers = [device(x, y, z + 1, c), device(x, y, z - 1, c), device(x, y + 1, z, c), device(x, y - 1, z, c), sib]
    for a in (-1, 1):
        for e in (0, 1):
            peers.append(device(x + a, y, z, e))
    peers += [device(x, y, z + 2, c), device(x, y, z - 2, c), device(x + 1 - 2 * p, y + 1 - 2 * ylo, z, c)]
    for dev in peers:
        pl.semaphore_signal(barrier, inc=1, device_id=dev, device_id_type=MESH)
    pl.semaphore_wait(barrier, len(peers))

    def p1(h, n):
        ref = slot(z, ds[h], h, n)
        return rcopy(ref, ref, p_s.at[h, n], p_r.at[h, n], device(x, y + (1 if h == 0 else -1), z, c))

    def ring(sign, h, k, n, incoming=False):
        zz = ring8(z - sign * (k if incoming else k - 1))
        j = 0 if sign > 0 else 1
        ref = slot(zz, ds[h], h, n)
        return rcopy(ref, ref, z_s.at[j, h, k - 1, n], z_r.at[j, h, k - 1, n], device(x, y, z + sign, c))

    def hops(sign, h):
        return 4 if (sign > 0) == (h == 0) else 3

    def yout(h, zz, n):
        ref = slot(zz, ds[h], h, n)
        return rcopy(ref, ref, y_s.at[h, zz, n], y_r.at[h, zz, n],
                     device(x, y + (sgn if h == 0 else -sgn), z, c))

    def yin(h, zz, n):
        ref = slot(zz, 1 - ds[h], h, n)
        return rcopy(ref, ref, y_s.at[h, zz, n], y_r.at[h, zz, n],
                     device(x, y + (sgn if h == 0 else -sgn), z, c))

    def xout(zz, j):
        pe = lax.rem(zz, 2)
        if j == 0:
            col = pl.multiple_of((zz * 2 + p) * 768 + (1 - c) * 384, 128)
            return rcopy(tok.at[0, :, pl.ds(col, 384)], X.at[zz, pl.ds(rows, rows), :],
                         x_s.at[zz, 0], x_r.at[zz, 0], sib)
        px = x + jnp.where(p == pe, 1, -1)
        e = j - 1
        col = pl.multiple_of((zz * 2 + 1 - p) * 768 + e * 384, 128)
        return rcopy(tok.at[0, :, pl.ds(col, 384)], X.at[zz, pl.ds((2 + c) * rows, rows), :],
                     x_s.at[zz, j], x_r.at[zz, 1 + c], device(px, y, z, e))

    def xin(zz, j):
        px = x + jnp.where(p == lax.rem(zz, 2), 1, -1)
        dst = X.at[zz, pl.ds((1 + j) * rows, rows), :]
        return rcopy(dst, dst, x_s.at[zz, j], x_r.at[zz, j], device(px, y, z, c))

    def start_x(t, _):
        zz = ring8(z + nth(t))
        for j in range(3):
            xout(zz, j).start()
        return 0

    def spread(h, n):
        for s in (1, -1):
            ring(s, h, 1, n).start()
        yout(h, z, n).start()

    def feed(ns):
        @pl.when(src)
        def _():
            for n in ns:
                for h in (0, 1):
                    p1(h, n).start()
            for n in ns:
                for h in (0, 1):
                    spread(h, n)

    def enter(ns):
        @pl.when(jnp.logical_not(src))
        def _():
            for n in ns:
                for h in (0, 1):
                    p1(h, n).wait_recv()
                    spread(h, n)

    def hop(k, ns):
        for n in ns:
            for h in (0, 1):
                for s in (1, -1):
                    if k <= hops(s, h):
                        ring(s, h, k, n, True).wait_recv()
                        if k < hops(s, h):
                            ring(s, h, k + 1, n).start()
                        yout(h, ring8(z - s * k), n).start()

    @pl.when(src)
    def _():
        own(0).wait()
        own(1).wait()

    feed((0, 1))
    lax.fori_loop(0, 8, start_x, 0)
    enter((0, 1))

    acc[...] = jnp.zeros_like(acc)
    row = lax.broadcasted_iota(jnp.int32, (128, 128), 0)
    blk0 = ((z * 2 + ylo) * 8 + x * 2 + c) * 2
    pos = jnp.where(row < 64, span[blk0], span[blk0 + 1]) * 64 + lax.rem(row, 64)
    angle = pos.astype(F32) * freq[...]
    cos_ref[...] = jnp.cos(angle)
    sin_ref[...] = jnp.where(lax.broadcasted_iota(jnp.int32, (128, 128), 1) < 64, -1.0, 1.0) * jnp.sin(angle)

    def add(part, zz, w):
        r = jnp.dot(X[zz], w, preferred_element_type=F32)
        acc[part, pl.ds(0, 256), :] += r[:256]
        acc[part, pl.ds(pl.multiple_of(256 + lax.rem(zz, 2) * 256, 256), 256), :] += r[256:]

    def mm1(zz):
        for n in (0, 1):
            for h in (0, 1):
                yin(h, zz, n).wait_recv()
        loc(zz).wait()
        for j in range(3):
            xin(zz, j).wait_recv()
        for d in (0, 1):
            add(1 - d, zz, W1[zz * 2 + d])

    def mm2(zz):
        for h in (0, 1):
            yin(h, zz, 2).wait_recv()
        add(2, zz, jnp.concatenate([W2[zz * 2], W2[zz * 2 + 1]], axis=1))

    def each(f, lo, hi):
        @functools.partial(lax.fori_loop, lo, hi, init_val=0)
        def _(t, _):
            f(ring8(z + nth(t)))
            return 0

    def d2d(j, part):
        blk = 128 if j == 0 else pl.multiple_of(256 * j + (1 - c) * 128, 128)
        return rcopy(acc.at[part, pl.ds(blk, 128), :], rsib.at[part, j], d_s.at[part, j], d_r.at[part, j], sib)

    def fin(pe, part):
        px = x + jnp.where(p == pe, 1, -1)
        return rcopy(psend.at[part, pe], precv.at[part, pe], f_s.at[part, pe], f_r.at[part, pe],
                     device(px, y, z, c))

    def to_sibling(part):
        for j in (1, 2, 0):
            d2d(j, part).start()

    def to_chips(part):
        for pe in (0, 1):
            d2d(pe + 1, part).wait_recv()
            mine = acc[part, pl.ds(pl.multiple_of(256 + pe * 256 + c * 128, 128), 128), :]
            psend[part, pe] = mine + rsib[part, pe + 1]
            fin(pe, part).start()

    def finish(part):
        d2d(0, part).wait_recv()
        total = acc[part, pl.ds(0, 128), :] + rsib[part, 0]
        for pe in (0, 1):
            fin(pe, part).wait_recv()
            total = total + precv[part, pe]
        return total

    def rot(v):
        return v * cos_ref[...] + pltpu.roll(v, 64, 1) * sin_ref[...]

    def mate(g):
        return device(x + lax.rem(g, 2) * (1 - 2 * p), y + (g // 2) * (1 - 2 * ylo), z, c)

    def qcopy(g, pr):
        return rcopy(QB.at[pr, 0, :, pl.ds(0, 256)], QB.at[pr, g // 2, :, pl.ds((g % 2) * 256, 256)],
                     q_s.at[pr, g - 1], q_r.at[pr, g - 1], mate(g))

    def make_queries(pr):
        total = finish(1 + pr)
        for hh in (0, 1):
            q = (rot(total[:, hh * HD:(hh + 1) * HD]) * HD ** (-0.5)).astype(BF16)
            QB[pr, 0, :, hh * 128:(hh + 1) * 128] = q.T
        for g in (3, 2, 1):
            qcopy(g, pr).start()

    def line(i, k, incoming=False):
        s = (1 - 2 * i) if k < 4 else s4
        far = (0, 1, 2, 1, 2)[k]
        zz = ring8(z - s * (k if incoming else k - far))
        ref = KV.at[zz, c, 0]
        return rcopy(ref, ref, l_s.at[i, k - 1], l_r.at[i, k - 1], device(x, y, z + s * far, c))

    def cross(zz):
        return rcopy(KV.at[zz, c, 0], KV.at[zz, c, 1], c_s.at[zz], c_r.at[zz], device(xk, y, z, c))

    def over(zz, n, incoming=False):
        ref = KV.at[zz, 1 - c if incoming else c, n]
        return rcopy(ref, ref, v_s.at[zz, n], v_r.at[zz, n], sib)

    def line1(i, k, incoming=False):
        s = 1 - 2 * i
        ref = KV.at[ring8(z - s * k) if incoming else z, c, 1]
        return rcopy(ref, ref, n_s.at[i, k - 1], n_r.at[i, k - 1], device(x, y, z + s * k, c))

    def arrived(i, k):
        line(i, k, True).wait_recv()
        zz = ring8(z - ((1 - 2 * i) if k < 4 else s4) * k)
        if k > 2:
            cross(zz).start()
        over(zz, 0).start()

    def arrived1(i, k):
        line1(i, k, True).wait_recv()
        over(ring8(z - (1 - 2 * i) * k), 1).start()

    def crossed(zz):
        cross(zz).wait_recv()
        over(zz, 1).start()

    ALL = (0, 512)

    def scores(zz, B, S, part=ALL):
        lo, hi = part
        S[:, lo:hi] = jnp.dot(KV[zz, :, :, 0].reshape(512, 128), QB[B // 2, B % 2, :, lo:hi],
                              preferred_element_type=F32)

    def soften(zz, B, S, Pb, part=ALL):
        lo, hi = part
        n512 = hi - lo
        qp = qpos[B % 2, :, lo:hi]

        def kpos(b):
            xx = x if b // 2 % 2 == 0 else xk
            return span[((zz * 2 + ylo) * 8 + xx * 2 + b // 4) * 2 + b % 2]
        mx = None
        for b in range(8):
            t = jnp.max(S[b * 64:(b + 1) * 64, lo:hi].reshape(8, 8, n512), axis=0)
            t = jnp.where(kpos(b) < qp, t, NEG)
            mx = t if mx is None else jnp.maximum(mx, t)
        old = m_acc[B, :, lo:hi]
        new = jnp.maximum(old, jnp.max(mx, axis=0, keepdims=True))
        scale = jnp.exp(old - new)
        ls = None
        for b in range(8):
            lim = jnp.where(kpos(b) < qp, new, -NEG)
            pb = jnp.exp(S[b * 64:(b + 1) * 64, lo:hi] - lim)
            t = jnp.sum(pb.reshape(8, 8, n512), axis=0)
            ls = t if ls is None else ls + t
            Pb[b * 64:(b + 1) * 64, lo:hi] = pb.astype(BF16)
        vv = jnp.concatenate([KV[zz, e, n, 1] for e in range(2) for n in range(2)], axis=1)
        m_acc[B, :, lo:hi] = new
        l_acc[B, :, lo:hi] = l_acc[B, :, lo:hi] * scale + jnp.sum(ls, axis=0, keepdims=True)
        o_acc[B, :, lo:hi] = o_acc[B, :, lo:hi] * scale + jnp.dot(vv, Pb[:, lo:hi], preferred_element_type=F32)

    def ready(zz):
        for n in (0, 1):
            over(zz, n, True).wait_recv()

    def prepare():
        lane = lax.broadcasted_iota(jnp.int32, (1, 512), 1)
        half = lax.rem(lane, 128) // 64
        for j in (0, 1):
            ps = []
            for g in (2 * j, 2 * j + 1):
                gx = x + (g % 2) * (1 - 2 * p)
                gy = ylo + (g // 2) * (1 - 2 * ylo)
                blk = ((z * 2 + gy) * 8 + gx * 2 + c) * 2
                ps.append(jnp.where(half == 0, span[blk], span[blk + 1]))
            qpos[j] = jnp.where(lane < 256, ps[0], ps[1])
        m_acc[...] = jnp.full((4, 1, 512), NEG, F32)
        l_acc[...] = jnp.zeros((4, 1, 512), F32)
        o_acc[...] = jnp.zeros((4, 128, 512), F32)

    def diagonal(pr):
        r = lax.broadcasted_iota(jnp.int32, (128, 256), 0)
        l = lax.rem(lax.broadcasted_iota(jnp.int32, (128, 256), 1), 128)
        ok = jnp.logical_and(r // 64 == l // 64, r <= l)
        sc = jnp.dot(KV[z, c, 0, 0], QB[pr, 0, :, 0:256], preferred_element_type=F32)
        sc = jnp.where(ok, sc, NEG)
        top = jnp.max(sc, axis=0, keepdims=True)
        pb = jnp.where(ok, jnp.exp(sc - top), 0.0)
        m_acc[2 * pr, :, 0:256] = top
        l_acc[2 * pr, :, 0:256] = jnp.sum(pb, axis=0, keepdims=True)
        o_acc[2 * pr, :, 0:256] = jnp.dot(KV[z, c, 0, 1], pb.astype(BF16), preferred_element_type=F32)

    def ocopy(g, pr):
        return rcopy(o_out.at[pr, g - 1], o_in.at[pr, g - 1], o_s.at[0, pr, g - 1], o_r.at[0, pr, g - 1], mate(g))

    def stcopy(g, pr):
        return rcopy(st_out.at[pr, g - 1], st_in.at[pr, g - 1], o_s.at[1, pr, g - 1], o_r.at[1, pr, g - 1], mate(g))

    def give(g, pr):
        B, lo = 2 * pr + g // 2, (g % 2) * 256
        l2 = l_acc[B, :, lo:lo + 256]
        o_out[pr, g - 1] = (o_acc[B, :, lo:lo + 256] * jnp.where(l2 > 0.0, 1.0 / l2, 0.0)).astype(BF16)
        st_out[pr, g - 1, 0:1, :] = m_acc[B, :, lo:lo + 256]
        st_out[pr, g - 1, 1:2, :] = l2
        ocopy(g, pr).start()
        stcopy(g, pr).start()

    def merge(pr):
        for g in (3, 2, 1):
            stcopy(g, pr).wait_recv()
            ocopy(g, pr).wait_recv()
        m0, l0 = m_acc[2 * pr, :, 0:256], l_acc[2 * pr, :, 0:256]
        top = m0
        for g in range(3):
            top = jnp.maximum(top, st_in[pr, g, 0:1, :])
        e0 = jnp.exp(m0 - top)
        ws = [st_in[pr, g, 1:2, :] * jnp.exp(st_in[pr, g, 0:1, :] - top) for g in range(3)]
        inv = 1.0 / (l0 * e0 + ws[0] + ws[1] + ws[2])
        res = o_acc[2 * pr, :, 0:256] * (e0 * inv)
        for g in range(3):
            res = res + o_in[pr, g].astype(F32) * (ws[g] * inv)
        for hh in (0, 1):
            h = 2 * pr + hh
            out[0, :, h * 128:(h + 1) * 128] = res[:, hh * 128:(hh + 1) * 128].T.astype(BF16)

    hop(1, (0, 1))
    hop(2, (0, 1))
    each(mm1, 0, 1)
    feed((2,))
    hop(3, (0, 1))
    each(mm1, 1, 3)
    enter((2,))
    hop(4, (0, 1))
    each(mm1, 3, 5)
    hop(1, (2,))
    each(mm1, 5, 8)
    to_sibling(0)
    to_sibling(1)
    hop(2, (2,))
    to_chips(0)
    to_chips(1)
    prepare()
    hop(3, (2,))

    kv = finish(0)
    KV[z, c, 0, 0] = rot(kv[:, :HD]).astype(BF16)
    KV[z, c, 0, 1] = kv[:, HD:].T.astype(BF16)
    for k in (1, 2):
        for i in (0, 1):
            line(i, k).start()
        if k == 1:
            cross(z).start()
            over(z, 0).start()
    hop(4, (2,))
    each(mm2, 0, 3)
    for i in (0, 1):
        arrived(i, 1)
    crossed(z)
    for k in (1, 2):
        for i in (0, 1):
            line1(i, k).start()
    make_queries(0)
    each(mm2, 3, 5)
    for i in (0, 1):
        arrived(i, 2)
    for i in (0, 1):
        line(i, 3).start()
    line(0, 4).start()
    each(mm2, 5, 8)
    to_sibling(2)
    to_chips(2)
    for i in (0, 1):
        arrived1(i, 1)
    diagonal(0)
    for g in (3, 2, 1):
        qcopy(g, 0).wait_recv()

    @functools.partial(lax.fori_loop, 0, 8, init_val=0)
    def _(t, _):
        @pl.when(t == 3)
        def _():
            make_queries(1)

        @pl.when(t == 2)
        def _():
            for i in (0, 1):
                arrived(i, 3)
            arrived(0, 4)

        @pl.when(t == 3)
        def _():
            for i in (0, 1):
                arrived1(i, 2)

        @pl.when(t == 5)
        def _():
            for k in (3, -3, 4):
                crossed(ring8(z + k))
        zz = ring8(z + nth(t))
        ready(zz)
        scores(zz, 1, S0)
        scores(zz, 0, S1)
        soften(zz, 1, S0, P0)
        soften(zz, 0, S1, P1)
        return 0

    for g in (3, 2, 1):
        give(g, 0)
    diagonal(1)
    for g in (3, 2, 1):
        qcopy(g, 1).wait_recv()

    def sweep(B, part=ALL):
        scores(z, B, S0, part)

        @functools.partial(lax.fori_loop, 0, 4, init_val=0)
        def _(t, _):
            za, zb, zc = [ring8(z + nth(lax.rem(2 * t + n, 8))) for n in range(3)]
            scores(zb, B, S1, part)
            soften(za, B, S0, P0, part)
            scores(zc, B, S0, part)
            soften(zb, B, S1, P1, part)
            return 0

    sweep(3)
    give(3, 1)
    give(2, 1)
    sweep(2, (256, 512))
    give(1, 1)
    sweep(2, (0, 256))
    merge(0)
    merge(1)

    for k in (0, 3, -3, 4):
        cross(ring8(z + k)).wait_send()
    for k in (1, 2):
        for i in (0, 1):
            line1(i, k).wait_send()
    @pl.when(src)
    def _():
        for h in (0, 1):
            for n in range(3):
                p1(h, n).wait_send()
    for h in (0, 1):
        for s in (1, -1):
            for k in range(1, hops(s, h) + 1):
                for n in range(3):
                    ring(s, h, k, n).wait_send()
    for part in range(3):
        for j in range(3):
            d2d(j, part).wait_send()
        for pe in (0, 1):
            fin(pe, part).wait_send()
    for pr in (0, 1):
        for g in (1, 2, 3):
            qcopy(g, pr).wait_send()
            ocopy(g, pr).wait_send()
            stcopy(g, pr).wait_send()
    for k in range(1, 5):
        for i in (0, 1):
            if k < 4 or i == 0:
                line(i, k).wait_send()

    @functools.partial(lax.fori_loop, 0, 8, init_val=0)
    def _(t, _):
        for h in (0, 1):
            for n in range(3):
                yout(h, t, n).wait_send()
        for j in range(3):
            xout(t, j).wait_send()
        for n in (0, 1):
            over(t, n).wait_send()
        return 0


def sublayer(tokens, wsh, freq, span):
    dma = pltpu.SemaphoreType.DMA
    vm = pl.BlockSpec(memory_space=pltpu.VMEM)
    return pl.pallas_call(
        sublayer_kernel,
        out_shape=jax.ShapeDtypeStruct((1, 128, 512), BF16),
        in_specs=[pl.BlockSpec(memory_space=pl.ANY)] * 2 + [vm] + [pl.BlockSpec(memory_space=pltpu.SMEM)],
        out_specs=vm,
        scratch_shapes=[
            pltpu.VMEM((8, 512, 384), BF16),
            pltpu.VMEM((16, 384, 256), BF16),
            pltpu.VMEM((16, 384, 128), BF16),
            pltpu.VMEM((3, 768, 256), F32),
            pltpu.VMEM((3, 3, 128, 256), F32),
            pltpu.VMEM((3, 2, 128, 256), F32),
            pltpu.VMEM((3, 2, 128, 256), F32),
            pltpu.VMEM((2, 2, 128, 512), BF16),
            pltpu.VMEM((8, 2, 2, 2, 128, 128), BF16),
            pltpu.VMEM((128, 128), F32),
            pltpu.VMEM((128, 128), F32),
            pltpu.VMEM((512, 512), F32),
            pltpu.VMEM((512, 512), F32),
            pltpu.VMEM((512, 512), BF16),
            pltpu.VMEM((512, 512), BF16),
            pltpu.VMEM((4, 128, 512), F32),
            pltpu.VMEM((4, 1, 512), F32),
            pltpu.VMEM((4, 1, 512), F32),
            pltpu.VMEM((2, 1, 512), jnp.int32),
            pltpu.VMEM((2, 3, 128, 256), BF16),
            pltpu.VMEM((2, 3, 128, 256), BF16),
            pltpu.VMEM((2, 3, 8, 256), F32),
            pltpu.VMEM((2, 3, 8, 256), F32),
            dma((8,)), dma((8, 3)), dma((8, 3)), dma((2,)),
            dma((2, 3)), dma((2, 3)), dma((2, 2, 4, 3)), dma((2, 2, 4, 3)), dma((2, 8, 3)), dma((2, 8, 3)),
            dma((3, 3)), dma((3, 3)), dma((3, 2)), dma((3, 2)),
            dma((2, 3)), dma((2, 3)), dma((2, 4)), dma((2, 4)), dma((2, 2)), dma((2, 2)), dma((8,)), dma((8,)),
            dma((8, 2)), dma((8, 2)), dma((2, 2, 3)), dma((2, 2, 3)),
        ],
        compiler_params=pltpu.CompilerParams(
            collective_id=0, has_side_effects=True, vmem_limit_bytes=56 * 2**20
        ),
    )(tokens, wsh, freq, span)


def per_device(tokens, qkv_weight, span_pos):
    index = lax.rem(lax.broadcasted_iota(jnp.int32, (1, 128), 1), 64).astype(F32)
    freq = 1000000.0 ** (-index * 2.0 / HD)
    return sublayer(tokens, qkv_weight, freq, span_pos)


def solution(mesh):
    in_specs = (P("doc", ("outer", "inner"), None), P("outer", "doc"), P())
    out_specs = P("doc", ("outer", "inner"), None)
    return jax.shard_map(
        per_device, mesh=mesh, in_specs=in_specs, out_specs=out_specs, check_vma=False
    )
```

```python
import functools
import jax
import jax.numpy as jnp
import numpy as np
from jax import lax
from jax.experimental import pallas as pl
from jax.experimental.pallas import tpu as pltpu
from jax.sharding import PartitionSpec as P

HD = 128
QH = 4
MESH = pl.DeviceIdType.MESH
F32 = jnp.float32
BF16 = jnp.bfloat16


def place():
    doc = lax.axis_index("doc")
    outer = lax.axis_index("outer")
    inner = lax.axis_index("inner")
    return inner // 2, doc * 2 + outer % 2, outer // 2, inner % 2


def device(x, y, z, c):
    x = lax.rem(x + 4, 4)
    y = lax.rem(y + 4, 4)
    z = lax.rem(z + 8, 8)
    return {"doc": y // 2, "outer": z * 2 + lax.rem(y, 2), "inner": x * 2 + c}


def nth(t):
    return ((t + 1) // 2) * (lax.rem(t, 2) * 2 - 1)


def rcopy(src, dst, ssem, rsem, dev):
    return pltpu.make_async_remote_copy(
        src_ref=src, dst_ref=dst, send_sem=ssem, recv_sem=rsem, device_id=dev, device_id_type=MESH
    )


def sublayer_kernel(
    tok, wsh, freq, span, out,
    X, W1, W2, acc, rsib, psend, precv, QB, KV, cos_ref, sin_ref, S0, S1, P0, P1,
    o_acc, m_acc, l_acc, qpos, o_out, o_in, st_out, st_in,
    x_loc, x_s, x_r, w_loc, p_s, p_r, z_s, z_r, y_s, y_r, d_s, d_r, f_s, f_r,
    q_s, q_r, l_s, l_r, n_s, n_r, c_s, c_r, v_s, v_r, o_s, o_r,
):
    x, y, z, c = place()
    p = lax.rem(x, 2)
    ylo = lax.rem(y, 2)
    src = ylo == p
    sgn = jnp.where(src, -1, 1)
    doc = y // 2
    d0 = jnp.where(src, doc, lax.rem(y + 3, 4) // 2)
    d1 = jnp.where(src, doc, lax.rem(y + 1, 4) // 2)
    ds = (d0, d1)
    rows = 128
    xk = lax.rem(x + 3 + 2 * p, 4)
    s4 = 1 - 2 * c
    sib = device(x, y, z, 1 - c)
    NEG = -1e30

    def ring8(v):
        return lax.rem(v + 16, 8)

    def slot(zz, d, h, n):
        if n < 2:
            return W1.at[zz * 2 + d, pl.ds(h * 192 + n * 96, 96), :]
        return W2.at[zz * 2 + d, pl.ds(h * 192, 192), :]

    def own(n):
        if n == 0:
            col = pl.multiple_of(doc * 128, 128)
            return pltpu.make_async_copy(
                wsh.at[pl.ds(c * 384, 384), pl.ds(col, 256)], W1.at[z * 2 + doc], w_loc.at[0])
        col = pl.multiple_of((1 - doc) * 256, 128)
        return pltpu.make_async_copy(
            wsh.at[pl.ds(c * 384, 384), pl.ds(col, 128)], W2.at[z * 2 + doc], w_loc.at[1])

    @pl.when(src)
    def _():
        own(0).start()
        own(1).start()

    def loc(zz):
        col = pl.multiple_of((zz * 2 + p) * 768 + c * 384, 128)
        return pltpu.make_async_copy(
            tok.at[0, :, pl.ds(col, 384)], X.at[zz, pl.ds(0, rows), :], x_loc.at[zz]
        )

    def start_loc(t, _):
        loc(ring8(z + nth(t))).start()
        return 0

    lax.fori_loop(0, 8, start_loc, 0)

    barrier = pltpu.get_barrier_semaphore()
    peers = [device(x, y, z + 1, c), device(x, y, z - 1, c), device(x, y + 1, z, c), device(x, y - 1, z, c), sib]
    for a in (-1, 1):
        for e in (0, 1):
            peers.append(device(x + a, y, z, e))
    peers += [device(x, y, z + 2, c), device(x, y, z - 2, c), device(x + 1 - 2 * p, y + 1 - 2 * ylo, z, c)]
    for dev in peers:
        pl.semaphore_signal(barrier, inc=1, device_id=dev, device_id_type=MESH)
    pl.semaphore_wait(barrier, len(peers))

    def p1(h, n):
        ref = slot(z, ds[h], h, n)
        return rcopy(ref, ref, p_s.at[h, n], p_r.at[h, n], device(x, y + (1 if h == 0 else -1), z, c))

    def ring(sign, h, k, n, incoming=False):
        zz = ring8(z - sign * (k if incoming else k - 1))
        j = 0 if sign > 0 else 1
        ref = slot(zz, ds[h], h, n)
        return rcopy(ref, ref, z_s.at[j, h, k - 1, n], z_r.at[j, h, k - 1, n], device(x, y, z + sign, c))

    def hops(sign, h):
        return 4 if (sign > 0) == (h == 0) else 3

    def yout(h, zz, n):
        ref = slot(zz, ds[h], h, n)
        return rcopy(ref, ref, y_s.at[h, zz, n], y_r.at[h, zz, n],
                     device(x, y + (sgn if h == 0 else -sgn), z, c))

    def yin(h, zz, n):
        ref = slot(zz, 1 - ds[h], h, n)
        return rcopy(ref, ref, y_s.at[h, zz, n], y_r.at[h, zz, n],
                     device(x, y + (sgn if h == 0 else -sgn), z, c))

    def xout(zz, j):
        pe = lax.rem(zz, 2)
        if j == 0:
            col = pl.multiple_of((zz * 2 + p) * 768 + (1 - c) * 384, 128)
            return rcopy(tok.at[0, :, pl.ds(col, 384)], X.at[zz, pl.ds(rows, rows), :],
                         x_s.at[zz, 0], x_r.at[zz, 0], sib)
        px = x + jnp.where(p == pe, 1, -1)
        e = j - 1
        col = pl.multiple_of((zz * 2 + 1 - p) * 768 + e * 384, 128)
        return rcopy(tok.at[0, :, pl.ds(col, 384)], X.at[zz, pl.ds((2 + c) * rows, rows), :],
                     x_s.at[zz, j], x_r.at[zz, 1 + c], device(px, y, z, e))

    def xin(zz, j):
        px = x + jnp.where(p == lax.rem(zz, 2), 1, -1)
        dst = X.at[zz, pl.ds((1 + j) * rows, rows), :]
        return rcopy(dst, dst, x_s.at[zz, j], x_r.at[zz, j], device(px, y, z, c))

    def start_x(t, _):
        zz = ring8(z + nth(t))
        for j in range(3):
            xout(zz, j).start()
        return 0

    def spread(h, n):
        for s in (1, -1):
            ring(s, h, 1, n).start()
        yout(h, z, n).start()

    def feed(ns):
        @pl.when(src)
        def _():
            for n in ns:
                for h in (0, 1):
                    p1(h, n).start()
            for n in ns:
                for h in (0, 1):
                    spread(h, n)

    def enter(ns):
        @pl.when(jnp.logical_not(src))
        def _():
            for n in ns:
                for h in (0, 1):
                    p1(h, n).wait_recv()
                    spread(h, n)

    def hop(k, ns):
        for n in ns:
            for h in (0, 1):
                for s in (1, -1):
                    if k <= hops(s, h):
                        ring(s, h, k, n, True).wait_recv()
                        if k < hops(s, h):
                            ring(s, h, k + 1, n).start()
                        yout(h, ring8(z - s * k), n).start()

    @pl.when(src)
    def _():
        own(0).wait()
        own(1).wait()

    feed((0, 1))
    lax.fori_loop(0, 8, start_x, 0)
    enter((0, 1))

    acc[...] = jnp.zeros_like(acc)
    row = lax.broadcasted_iota(jnp.int32, (128, 128), 0)
    blk0 = ((z * 2 + ylo) * 8 + x * 2 + c) * 2
    pos = jnp.where(row < 64, span[blk0], span[blk0 + 1]) * 64 + lax.rem(row, 64)
    angle = pos.astype(F32) * freq[...]
    cos_ref[...] = jnp.cos(angle)
    sin_ref[...] = jnp.where(lax.broadcasted_iota(jnp.int32, (128, 128), 1) < 64, -1.0, 1.0) * jnp.sin(angle)

    def add(part, zz, w):
        r = jnp.dot(X[zz], w, preferred_element_type=F32)
        acc[part, pl.ds(0, 256), :] += r[:256]
        acc[part, pl.ds(pl.multiple_of(256 + lax.rem(zz, 2) * 256, 256), 256), :] += r[256:]

    def mm1(zz):
        for n in (0, 1):
            for h in (0, 1):
                yin(h, zz, n).wait_recv()
        loc(zz).wait()
        for j in range(3):
            xin(zz, j).wait_recv()
        for d in (0, 1):
            add(1 - d, zz, W1[zz * 2 + d])

    def mm2(zz):
        for h in (0, 1):
            yin(h, zz, 2).wait_recv()
        add(2, zz, jnp.concatenate([W2[zz * 2], W2[zz * 2 + 1]], axis=1))

    def each(f, lo, hi):
        @functools.partial(lax.fori_loop, lo, hi, init_val=0)
        def _(t, _):
            f(ring8(z + nth(t)))
            return 0

    def d2d(j, part):
        blk = 128 if j == 0 else pl.multiple_of(256 * j + (1 - c) * 128, 128)
        return rcopy(acc.at[part, pl.ds(blk, 128), :], rsib.at[part, j], d_s.at[part, j], d_r.at[part, j], sib)

    def fin(pe, part):
        px = x + jnp.where(p == pe, 1, -1)
        return rcopy(psend.at[part, pe], precv.at[part, pe], f_s.at[part, pe], f_r.at[part, pe],
                     device(px, y, z, c))

    def to_sibling(part):
        for j in (1, 2, 0):
            d2d(j, part).start()

    def to_chips(part):
        for pe in (0, 1):
            d2d(pe + 1, part).wait_recv()
            mine = acc[part, pl.ds(pl.multiple_of(256 + pe * 256 + c * 128, 128), 128), :]
            psend[part, pe] = mine + rsib[part, pe + 1]
            fin(pe, part).start()

    def finish(part):
        d2d(0, part).wait_recv()
        total = acc[part, pl.ds(0, 128), :] + rsib[part, 0]
        for pe in (0, 1):
            fin(pe, part).wait_recv()
            total = total + precv[part, pe]
        return total

    def rot(v):
        return v * cos_ref[...] + pltpu.roll(v, 64, 1) * sin_ref[...]

    def mate(g):
        return device(x + lax.rem(g, 2) * (1 - 2 * p), y + (g // 2) * (1 - 2 * ylo), z, c)

    def qcopy(g, pr):
        return rcopy(QB.at[pr, 0, :, pl.ds(0, 256)], QB.at[pr, g // 2, :, pl.ds((g % 2) * 256, 256)],
                     q_s.at[pr, g - 1], q_r.at[pr, g - 1], mate(g))

    def make_queries(pr):
        total = finish(1 + pr)
        for hh in (0, 1):
            q = (rot(total[:, hh * HD:(hh + 1) * HD]) * HD ** (-0.5)).astype(BF16)
            QB[pr, 0, :, hh * 128:(hh + 1) * 128] = q.T
        for g in (3, 2, 1):
            qcopy(g, pr).start()

    def line(i, k, incoming=False):
        s = (1 - 2 * i) if k < 4 else s4
        far = (0, 1, 2, 1, 2)[k]
        zz = ring8(z - s * (k if incoming else k - far))
        ref = KV.at[zz, c, 0]
        return rcopy(ref, ref, l_s.at[i, k - 1], l_r.at[i, k - 1], device(x, y, z + s * far, c))

    def cross(zz):
        return rcopy(KV.at[zz, c, 0], KV.at[zz, c, 1], c_s.at[zz], c_r.at[zz], device(xk, y, z, c))

    def over(zz, n, incoming=False):
        ref = KV.at[zz, 1 - c if incoming else c, n]
        return rcopy(ref, ref, v_s.at[zz, n], v_r.at[zz, n], sib)

    def line1(i, k, incoming=False):
        s = 1 - 2 * i
        ref = KV.at[ring8(z - s * k) if incoming else z, c, 1]
        return rcopy(ref, ref, n_s.at[i, k - 1], n_r.at[i, k - 1], device(x, y, z + s * k, c))

    def arrived(i, k):
        line(i, k, True).wait_recv()
        zz = ring8(z - ((1 - 2 * i) if k < 4 else s4) * k)
        if k > 2:
            cross(zz).start()
        over(zz, 0).start()

    def arrived1(i, k):
        line1(i, k, True).wait_recv()
        over(ring8(z - (1 - 2 * i) * k), 1).start()

    def crossed(zz):
        cross(zz).wait_recv()
        over(zz, 1).start()

    ALL = (0, 512)

    def scores(zz, B, S, part=ALL):
        lo, hi = part
        S[:, lo:hi] = jnp.dot(KV[zz, :, :, 0].reshape(512, 128), QB[B // 2, B % 2, :, lo:hi],
                              preferred_element_type=F32)

    def soften(zz, B, S, Pb, part=ALL):
        lo, hi = part
        n512 = hi - lo
        qp = qpos[B % 2, :, lo:hi]

        def kpos(b):
            xx = x if b // 2 % 2 == 0 else xk
            return span[((zz * 2 + ylo) * 8 + xx * 2 + b // 4) * 2 + b % 2]
        mx = None
        for b in range(8):
            t = jnp.max(S[b * 64:(b + 1) * 64, lo:hi].reshape(8, 8, n512), axis=0)
            t = jnp.where(kpos(b) < qp, t, NEG)
            mx = t if mx is None else jnp.maximum(mx, t)
        old = m_acc[B, :, lo:hi]
        new = jnp.maximum(old, jnp.max(mx, axis=0, keepdims=True))
        scale = jnp.exp(old - new)
        ls = None
        for b in range(8):
            lim = jnp.where(kpos(b) < qp, new, -NEG)
            pb = jnp.exp(S[b * 64:(b + 1) * 64, lo:hi] - lim)
            t = jnp.sum(pb.reshape(8, 8, n512), axis=0)
            ls = t if ls is None else ls + t
            Pb[b * 64:(b + 1) * 64, lo:hi] = pb.astype(BF16)
        vv = jnp.concatenate([KV[zz, e, n, 1] for e in range(2) for n in range(2)], axis=1)
        m_acc[B, :, lo:hi] = new
        l_acc[B, :, lo:hi] = l_acc[B, :, lo:hi] * scale + jnp.sum(ls, axis=0, keepdims=True)
        o_acc[B, :, lo:hi] = o_acc[B, :, lo:hi] * scale + jnp.dot(vv, Pb[:, lo:hi], preferred_element_type=F32)

    def ready(zz):
        for n in (0, 1):
            over(zz, n, True).wait_recv()

    def prepare():
        lane = lax.broadcasted_iota(jnp.int32, (1, 512), 1)
        half = lax.rem(lane, 128) // 64
        for j in (0, 1):
            ps = []
            for g in (2 * j, 2 * j + 1):
                gx = x + (g % 2) * (1 - 2 * p)
                gy = ylo + (g // 2) * (1 - 2 * ylo)
                blk = ((z * 2 + gy) * 8 + gx * 2 + c) * 2
                ps.append(jnp.where(half == 0, span[blk], span[blk + 1]))
            qpos[j] = jnp.where(lane < 256, ps[0], ps[1])
        m_acc[...] = jnp.full((4, 1, 512), NEG, F32)
        l_acc[...] = jnp.zeros((4, 1, 512), F32)
        o_acc[...] = jnp.zeros((4, 128, 512), F32)

    def diagonal(pr):
        r = lax.broadcasted_iota(jnp.int32, (128, 256), 0)
        l = lax.rem(lax.broadcasted_iota(jnp.int32, (128, 256), 1), 128)
        ok = jnp.logical_and(r // 64 == l // 64, r <= l)
        sc = jnp.dot(KV[z, c, 0, 0], QB[pr, 0, :, 0:256], preferred_element_type=F32)
        sc = jnp.where(ok, sc, NEG)
        top = jnp.max(sc, axis=0, keepdims=True)
        pb = jnp.where(ok, jnp.exp(sc - top), 0.0)
        m_acc[2 * pr, :, 0:256] = top
        l_acc[2 * pr, :, 0:256] = jnp.sum(pb, axis=0, keepdims=True)
        o_acc[2 * pr, :, 0:256] = jnp.dot(KV[z, c, 0, 1], pb.astype(BF16), preferred_element_type=F32)

    def ocopy(g, pr):
        return rcopy(o_out.at[pr, g - 1], o_in.at[pr, g - 1], o_s.at[0, pr, g - 1], o_r.at[0, pr, g - 1], mate(g))

    def stcopy(g, pr):
        return rcopy(st_out.at[pr, g - 1], st_in.at[pr, g - 1], o_s.at[1, pr, g - 1], o_r.at[1, pr, g - 1], mate(g))

    def give(g, pr):
        B, lo = 2 * pr + g // 2, (g % 2) * 256
        l2 = l_acc[B, :, lo:lo + 256]
        o_out[pr, g - 1] = (o_acc[B, :, lo:lo + 256] * jnp.where(l2 > 0.0, 1.0 / l2, 0.0)).astype(BF16)
        st_out[pr, g - 1, 0:1, :] = m_acc[B, :, lo:lo + 256]
        st_out[pr, g - 1, 1:2, :] = l2
        stcopy(g, pr).start()
        ocopy(g, pr).start()

    def merge(pr):
        for g in (3, 2, 1):
            stcopy(g, pr).wait_recv()
        m0, l0 = m_acc[2 * pr, :, 0:256], l_acc[2 * pr, :, 0:256]
        top = m0
        for g in range(3):
            top = jnp.maximum(top, st_in[pr, g, 0:1, :])
        e0 = jnp.exp(m0 - top)
        ws = [st_in[pr, g, 1:2, :] * jnp.exp(st_in[pr, g, 0:1, :] - top) for g in range(3)]
        inv = 1.0 / (l0 * e0 + ws[0] + ws[1] + ws[2])
        res = o_acc[2 * pr, :, 0:256] * (e0 * inv)
        for g in (3, 2, 1):
            ocopy(g, pr).wait_recv()
        for g in range(3):
            res = res + o_in[pr, g].astype(F32) * (ws[g] * inv)
        for hh in (0, 1):
            h = 2 * pr + hh
            out[0, :, h * 128:(h + 1) * 128] = res[:, hh * 128:(hh + 1) * 128].T.astype(BF16)

    hop(1, (0, 1))
    hop(2, (0, 1))
    each(mm1, 0, 1)
    feed((2,))
    hop(3, (0, 1))
    each(mm1, 1, 3)
    enter((2,))
    hop(4, (0, 1))
    each(mm1, 3, 5)
    hop(1, (2,))
    each(mm1, 5, 8)
    to_sibling(0)
    to_sibling(1)
    hop(2, (2,))
    to_chips(0)
    to_chips(1)
    prepare()
    hop(3, (2,))

    kv = finish(0)
    KV[z, c, 0, 0] = rot(kv[:, :HD]).astype(BF16)
    KV[z, c, 0, 1] = kv[:, HD:].T.astype(BF16)
    for k in (1, 2):
        for i in (0, 1):
            line(i, k).start()
        if k == 1:
            cross(z).start()
            over(z, 0).start()
    hop(4, (2,))
    each(mm2, 0, 3)
    for i in (0, 1):
        arrived(i, 1)
    crossed(z)
    for k in (1, 2):
        for i in (0, 1):
            line1(i, k).start()
    make_queries(0)
    each(mm2, 3, 5)
    for i in (0, 1):
        arrived(i, 2)
    for i in (0, 1):
        line(i, 3).start()
    line(0, 4).start()
    each(mm2, 5, 8)
    to_sibling(2)
    to_chips(2)
    for i in (0, 1):
        arrived1(i, 1)
    diagonal(0)
    for g in (3, 2, 1):
        qcopy(g, 0).wait_recv()

    @functools.partial(lax.fori_loop, 0, 8, init_val=0)
    def _(t, _):
        @pl.when(t == 3)
        def _():
            make_queries(1)

        @pl.when(t == 2)
        def _():
            for i in (0, 1):
                arrived(i, 3)
            arrived(0, 4)

        @pl.when(t == 3)
        def _():
            for i in (0, 1):
                arrived1(i, 2)

        @pl.when(t == 5)
        def _():
            for k in (3, -3, 4):
                crossed(ring8(z + k))
        zz = ring8(z + nth(t))
        ready(zz)
        scores(zz, 1, S0)
        scores(zz, 0, S1)
        soften(zz, 1, S0, P0)
        soften(zz, 0, S1, P1)
        return 0

    for g in (3, 2, 1):
        give(g, 0)
    diagonal(1)
    for g in (3, 2, 1):
        qcopy(g, 1).wait_recv()

    def sweep(B, part=ALL):
        scores(z, B, S0, part)

        @functools.partial(lax.fori_loop, 0, 4, init_val=0)
        def _(t, _):
            za, zb, zc = [ring8(z + nth(lax.rem(2 * t + n, 8))) for n in range(3)]
            scores(zb, B, S1, part)
            soften(za, B, S0, P0, part)
            scores(zc, B, S0, part)
            soften(zb, B, S1, P1, part)
            return 0

    sweep(3)
    give(3, 1)
    give(2, 1)
    sweep(2, (256, 512))
    give(1, 1)
    sweep(2, (0, 256))
    merge(0)
    merge(1)

    for k in (0, 3, -3, 4):
        cross(ring8(z + k)).wait_send()
    for k in (1, 2):
        for i in (0, 1):
            line1(i, k).wait_send()
    @pl.when(src)
    def _():
        for h in (0, 1):
            for n in range(3):
                p1(h, n).wait_send()
    for h in (0, 1):
        for s in (1, -1):
            for k in range(1, hops(s, h) + 1):
                for n in range(3):
                    ring(s, h, k, n).wait_send()
    for part in range(3):
        for j in range(3):
            d2d(j, part).wait_send()
        for pe in (0, 1):
            fin(pe, part).wait_send()
    for pr in (0, 1):
        for g in (1, 2, 3):
            qcopy(g, pr).wait_send()
            ocopy(g, pr).wait_send()
            stcopy(g, pr).wait_send()
    for k in range(1, 5):
        for i in (0, 1):
            if k < 4 or i == 0:
                line(i, k).wait_send()

    @functools.partial(lax.fori_loop, 0, 8, init_val=0)
    def _(t, _):
        for h in (0, 1):
            for n in range(3):
                yout(h, t, n).wait_send()
        for j in range(3):
            xout(t, j).wait_send()
        for n in (0, 1):
            over(t, n).wait_send()
        return 0


def sublayer(tokens, wsh, freq, span):
    dma = pltpu.SemaphoreType.DMA
    vm = pl.BlockSpec(memory_space=pltpu.VMEM)
    return pl.pallas_call(
        sublayer_kernel,
        out_shape=jax.ShapeDtypeStruct((1, 128, 512), BF16),
        in_specs=[pl.BlockSpec(memory_space=pl.ANY)] * 2 + [vm] + [pl.BlockSpec(memory_space=pltpu.SMEM)],
        out_specs=vm,
        scratch_shapes=[
            pltpu.VMEM((8, 512, 384), BF16),
            pltpu.VMEM((16, 384, 256), BF16),
            pltpu.VMEM((16, 384, 128), BF16),
            pltpu.VMEM((3, 768, 256), F32),
            pltpu.VMEM((3, 3, 128, 256), F32),
            pltpu.VMEM((3, 2, 128, 256), F32),
            pltpu.VMEM((3, 2, 128, 256), F32),
            pltpu.VMEM((2, 2, 128, 512), BF16),
            pltpu.VMEM((8, 2, 2, 2, 128, 128), BF16),
            pltpu.VMEM((128, 128), F32),
            pltpu.VMEM((128, 128), F32),
            pltpu.VMEM((512, 512), F32),
            pltpu.VMEM((512, 512), F32),
            pltpu.VMEM((512, 512), BF16),
            pltpu.VMEM((512, 512), BF16),
            pltpu.VMEM((4, 128, 512), F32),
            pltpu.VMEM((4, 1, 512), F32),
            pltpu.VMEM((4, 1, 512), F32),
            pltpu.VMEM((2, 1, 512), jnp.int32),
            pltpu.VMEM((2, 3, 128, 256), BF16),
            pltpu.VMEM((2, 3, 128, 256), BF16),
            pltpu.VMEM((2, 3, 8, 256), F32),
            pltpu.VMEM((2, 3, 8, 256), F32),
            dma((8,)), dma((8, 3)), dma((8, 3)), dma((2,)),
            dma((2, 3)), dma((2, 3)), dma((2, 2, 4, 3)), dma((2, 2, 4, 3)), dma((2, 8, 3)), dma((2, 8, 3)),
            dma((3, 3)), dma((3, 3)), dma((3, 2)), dma((3, 2)),
            dma((2, 3)), dma((2, 3)), dma((2, 4)), dma((2, 4)), dma((2, 2)), dma((2, 2)), dma((8,)), dma((8,)),
            dma((8, 2)), dma((8, 2)), dma((2, 2, 3)), dma((2, 2, 3)),
        ],
        compiler_params=pltpu.CompilerParams(
            collective_id=0, has_side_effects=True, vmem_limit_bytes=56 * 2**20
        ),
    )(tokens, wsh, freq, span)


def per_device(tokens, qkv_weight, span_pos):
    index = np.arange(128, dtype=np.int64)[None, :] % 64
    freq = jnp.asarray((1000000.0 ** (-index * 2.0 / HD)).astype(np.float32))
    return sublayer(tokens, qkv_weight, freq, span_pos)


def solution(mesh):
    in_specs = (P("doc", ("outer", "inner"), None), P("outer", "doc"), P())
    out_specs = P("doc", ("outer", "inner"), None)
    return jax.shard_map(
        per_device, mesh=mesh, in_specs=in_specs, out_specs=out_specs, check_vma=False
    )
```

```python
import functools
import jax
import jax.numpy as jnp
import numpy as np
from jax import lax
from jax.experimental import pallas as pl
from jax.experimental.pallas import tpu as pltpu
from jax.sharding import PartitionSpec as P

HD = 128
QH = 4
MESH = pl.DeviceIdType.MESH
F32 = jnp.float32
BF16 = jnp.bfloat16


def place():
    doc = lax.axis_index("doc")
    outer = lax.axis_index("outer")
    inner = lax.axis_index("inner")
    return inner // 2, doc * 2 + outer % 2, outer // 2, inner % 2


def device(x, y, z, c):
    x = lax.rem(x + 4, 4)
    y = lax.rem(y + 4, 4)
    z = lax.rem(z + 8, 8)
    return {"doc": y // 2, "outer": z * 2 + lax.rem(y, 2), "inner": x * 2 + c}


def nth(t):
    return ((t + 1) // 2) * (lax.rem(t, 2) * 2 - 1)


def rcopy(src, dst, ssem, rsem, dev):
    return pltpu.make_async_remote_copy(
        src_ref=src, dst_ref=dst, send_sem=ssem, recv_sem=rsem, device_id=dev, device_id_type=MESH
    )


def sublayer_kernel(
    tok, wsh, freq, span, out,
    X, W1, W2, acc, rsib, psend, precv, QB, KV, cos_ref, sin_ref, S0, S1, P0, P1,
    o_acc, m_acc, l_acc, qpos, o_out, o_in, st_out, st_in,
    x_loc, x_s, x_r, w_loc, p_s, p_r, z_s, z_r, y_s, y_r, d_s, d_r, f_s, f_r,
    q_s, q_r, l_s, l_r, n_s, n_r, c_s, c_r, v_s, v_r, o_s, o_r,
):
    x, y, z, c = place()
    p = lax.rem(x, 2)
    ylo = lax.rem(y, 2)
    src = ylo == p
    sgn = jnp.where(src, -1, 1)
    doc = y // 2
    d0 = jnp.where(src, doc, lax.rem(y + 3, 4) // 2)
    d1 = jnp.where(src, doc, lax.rem(y + 1, 4) // 2)
    ds = (d0, d1)
    rows = 128
    xk = lax.rem(x + 3 + 2 * p, 4)
    s4 = 1 - 2 * c
    sib = device(x, y, z, 1 - c)
    NEG = -1e30

    def ring8(v):
        return lax.rem(v + 16, 8)

    def slot(zz, d, h, n):
        if n < 2:
            return W1.at[zz * 2 + d, pl.ds(h * 192 + n * 96, 96), :]
        return W2.at[zz * 2 + d, pl.ds(h * 192, 192), :]

    def own(n):
        if n == 0:
            col = pl.multiple_of(doc * 128, 128)
            return pltpu.make_async_copy(
                wsh.at[pl.ds(c * 384, 384), pl.ds(col, 256)], W1.at[z * 2 + doc], w_loc.at[0])
        col = pl.multiple_of((1 - doc) * 256, 128)
        return pltpu.make_async_copy(
            wsh.at[pl.ds(c * 384, 384), pl.ds(col, 128)], W2.at[z * 2 + doc], w_loc.at[1])

    @pl.when(src)
    def _():
        own(0).start()
        own(1).start()

    def loc(zz):
        col = pl.multiple_of((zz * 2 + p) * 768 + c * 384, 128)
        return pltpu.make_async_copy(
            tok.at[0, :, pl.ds(col, 384)], X.at[zz, pl.ds(0, rows), :], x_loc.at[zz]
        )

    def start_loc(t, _):
        loc(ring8(z + nth(t))).start()
        return 0

    lax.fori_loop(0, 8, start_loc, 0)

    barrier = pltpu.get_barrier_semaphore()
    peers = [device(x, y, z + 1, c), device(x, y, z - 1, c), device(x, y + 1, z, c), device(x, y - 1, z, c), sib]
    for a in (-1, 1):
        for e in (0, 1):
            peers.append(device(x + a, y, z, e))
    peers += [device(x, y, z + 2, c), device(x, y, z - 2, c), device(x + 1 - 2 * p, y + 1 - 2 * ylo, z, c)]
    for dev in peers:
        pl.semaphore_signal(barrier, inc=1, device_id=dev, device_id_type=MESH)
    pl.semaphore_wait(barrier, len(peers))

    def p1(h, n):
        ref = slot(z, ds[h], h, n)
        return rcopy(ref, ref, p_s.at[h, n], p_r.at[h, n], device(x, y + (1 if h == 0 else -1), z, c))

    def ring(sign, h, k, n, incoming=False):
        zz = ring8(z - sign * (k if incoming else k - 1))
        j = 0 if sign > 0 else 1
        ref = slot(zz, ds[h], h, n)
        return rcopy(ref, ref, z_s.at[j, h, k - 1, n], z_r.at[j, h, k - 1, n], device(x, y, z + sign, c))

    def hops(sign, h):
        return 4 if (sign > 0) == (h == 0) else 3

    def yout(h, zz, n):
        ref = slot(zz, ds[h], h, n)
        return rcopy(ref, ref, y_s.at[h, zz, n], y_r.at[h, zz, n],
                     device(x, y + (sgn if h == 0 else -sgn), z, c))

    def yin(h, zz, n):
        ref = slot(zz, 1 - ds[h], h, n)
        return rcopy(ref, ref, y_s.at[h, zz, n], y_r.at[h, zz, n],
                     device(x, y + (sgn if h == 0 else -sgn), z, c))

    def xout(zz, j):
        pe = lax.rem(zz, 2)
        if j == 0:
            col = pl.multiple_of((zz * 2 + p) * 768 + (1 - c) * 384, 128)
            return rcopy(tok.at[0, :, pl.ds(col, 384)], X.at[zz, pl.ds(rows, rows), :],
                         x_s.at[zz, 0], x_r.at[zz, 0], sib)
        px = x + jnp.where(p == pe, 1, -1)
        e = j - 1
        col = pl.multiple_of((zz * 2 + 1 - p) * 768 + e * 384, 128)
        return rcopy(tok.at[0, :, pl.ds(col, 384)], X.at[zz, pl.ds((2 + c) * rows, rows), :],
                     x_s.at[zz, j], x_r.at[zz, 1 + c], device(px, y, z, e))

    def xin(zz, j):
        px = x + jnp.where(p == lax.rem(zz, 2), 1, -1)
        dst = X.at[zz, pl.ds((1 + j) * rows, rows), :]
        return rcopy(dst, dst, x_s.at[zz, j], x_r.at[zz, j], device(px, y, z, c))

    def start_x(t, _):
        zz = ring8(z + nth(t))
        for j in range(3):
            xout(zz, j).start()
        return 0

    def spread(h, n):
        for s in (1, -1):
            ring(s, h, 1, n).start()
        yout(h, z, n).start()

    def feed(ns):
        @pl.when(src)
        def _():
            for n in ns:
                for h in (0, 1):
                    p1(h, n).start()
            for n in ns:
                for h in (0, 1):
                    spread(h, n)

    def enter(ns):
        @pl.when(jnp.logical_not(src))
        def _():
            for n in ns:
                for h in (0, 1):
                    p1(h, n).wait_recv()
                    spread(h, n)

    def hop(k, ns):
        for n in ns:
            for h in (0, 1):
                for s in (1, -1):
                    if k <= hops(s, h):
                        ring(s, h, k, n, True).wait_recv()
                        if k < hops(s, h):
                            ring(s, h, k + 1, n).start()
                        yout(h, ring8(z - s * k), n).start()

    @pl.when(src)
    def _():
        own(0).wait()
        own(1).wait()

    feed((0, 1))
    lax.fori_loop(0, 8, start_x, 0)
    enter((0, 1))

    acc[...] = jnp.zeros_like(acc)
    row = lax.broadcasted_iota(jnp.int32, (128, 128), 0)
    blk0 = ((z * 2 + ylo) * 8 + x * 2 + c) * 2
    pos = jnp.where(row < 64, span[blk0], span[blk0 + 1]) * 64 + lax.rem(row, 64)
    angle = pos.astype(F32) * freq[...]
    cos_ref[...] = jnp.cos(angle)
    sin_ref[...] = jnp.where(lax.broadcasted_iota(jnp.int32, (128, 128), 1) < 64, -1.0, 1.0) * jnp.sin(angle)

    def add(part, zz, w):
        r = jnp.dot(X[zz], w, preferred_element_type=F32)
        acc[part, pl.ds(0, 256), :] += r[:256]
        acc[part, pl.ds(pl.multiple_of(256 + lax.rem(zz, 2) * 256, 256), 256), :] += r[256:]

    def mm1(zz):
        for n in (0, 1):
            for h in (0, 1):
                yin(h, zz, n).wait_recv()
        loc(zz).wait()
        for j in range(3):
            xin(zz, j).wait_recv()
        for d in (0, 1):
            add(1 - d, zz, W1[zz * 2 + d])

    def mm2(zz):
        for h in (0, 1):
            yin(h, zz, 2).wait_recv()
        add(2, zz, jnp.concatenate([W2[zz * 2], W2[zz * 2 + 1]], axis=1))

    def each(f, lo, hi):
        @functools.partial(lax.fori_loop, lo, hi, init_val=0)
        def _(t, _):
            f(ring8(z + nth(t)))
            return 0

    def d2d(j, part):
        blk = 128 if j == 0 else pl.multiple_of(256 * j + (1 - c) * 128, 128)
        return rcopy(acc.at[part, pl.ds(blk, 128), :], rsib.at[part, j], d_s.at[part, j], d_r.at[part, j], sib)

    def fin(pe, part):
        px = x + jnp.where(p == pe, 1, -1)
        return rcopy(psend.at[part, pe], precv.at[part, pe], f_s.at[part, pe], f_r.at[part, pe],
                     device(px, y, z, c))

    def to_sibling(part):
        for j in (1, 2, 0):
            d2d(j, part).start()

    def to_chips(part):
        for pe in (0, 1):
            d2d(pe + 1, part).wait_recv()
            mine = acc[part, pl.ds(pl.multiple_of(256 + pe * 256 + c * 128, 128), 128), :]
            psend[part, pe] = mine + rsib[part, pe + 1]
            fin(pe, part).start()

    def finish(part):
        d2d(0, part).wait_recv()
        total = acc[part, pl.ds(0, 128), :] + rsib[part, 0]
        for pe in (0, 1):
            fin(pe, part).wait_recv()
            total = total + precv[part, pe]
        return total

    def rot(v):
        return v * cos_ref[...] + pltpu.roll(v, 64, 1) * sin_ref[...]

    def mate(g):
        return device(x + lax.rem(g, 2) * (1 - 2 * p), y + (g // 2) * (1 - 2 * ylo), z, c)

    def qcopy(g, pr):
        return rcopy(QB.at[pr, 0, :, pl.ds(0, 256)], QB.at[pr, g // 2, :, pl.ds((g % 2) * 256, 256)],
                     q_s.at[pr, g - 1], q_r.at[pr, g - 1], mate(g))

    def make_queries(pr):
        total = finish(1 + pr)
        for hh in (0, 1):
            q = (rot(total[:, hh * HD:(hh + 1) * HD]) * HD ** (-0.5)).astype(BF16)
            QB[pr, 0, :, hh * 128:(hh + 1) * 128] = q.T
        for g in (3, 2, 1):
            qcopy(g, pr).start()

    def line(i, k, incoming=False):
        s = (1 - 2 * i) if k < 4 else s4
        far = (0, 1, 2, 1, 2)[k]
        zz = ring8(z - s * (k if incoming else k - far))
        ref = KV.at[zz, c, 0]
        return rcopy(ref, ref, l_s.at[i, k - 1], l_r.at[i, k - 1], device(x, y, z + s * far, c))

    def cross(zz):
        return rcopy(KV.at[zz, c, 0], KV.at[zz, c, 1], c_s.at[zz], c_r.at[zz], device(xk, y, z, c))

    def over(zz, n, incoming=False):
        ref = KV.at[zz, 1 - c if incoming else c, n]
        return rcopy(ref, ref, v_s.at[zz, n], v_r.at[zz, n], sib)

    def line1(i, k, incoming=False):
        s = 1 - 2 * i
        ref = KV.at[ring8(z - s * k) if incoming else z, c, 1]
        return rcopy(ref, ref, n_s.at[i, k - 1], n_r.at[i, k - 1], device(x, y, z + s * k, c))

    def arrived(i, k):
        line(i, k, True).wait_recv()
        zz = ring8(z - ((1 - 2 * i) if k < 4 else s4) * k)
        if k > 2:
            cross(zz).start()
        over(zz, 0).start()

    def arrived1(i, k):
        line1(i, k, True).wait_recv()
        over(ring8(z - (1 - 2 * i) * k), 1).start()

    def crossed(zz):
        cross(zz).wait_recv()
        over(zz, 1).start()

    ALL = (0, 512)

    def scores(zz, B, S, part=ALL):
        lo, hi = part
        S[:, lo:hi] = jnp.dot(KV[zz, :, :, 0].reshape(512, 128), QB[B // 2, B % 2, :, lo:hi],
                              preferred_element_type=F32)

    def soften(zz, B, S, Pb, part=ALL):
        lo, hi = part
        n512 = hi - lo
        qp = qpos[B % 2, :, lo:hi]

        def kpos(b):
            xx = x if b // 2 % 2 == 0 else xk
            return span[((zz * 2 + ylo) * 8 + xx * 2 + b // 4) * 2 + b % 2]
        mx = None
        for b in range(8):
            t = jnp.max(S[b * 64:(b + 1) * 64, lo:hi].reshape(8, 8, n512), axis=0)
            t = jnp.where(kpos(b) < qp, t, NEG)
            mx = t if mx is None else jnp.maximum(mx, t)
        old = m_acc[B, :, lo:hi]
        new = jnp.maximum(old, jnp.max(mx, axis=0, keepdims=True))
        scale = jnp.exp(old - new)
        ls = None
        for b in range(8):
            lim = jnp.where(kpos(b) < qp, new, -NEG)
            pb = jnp.exp(S[b * 64:(b + 1) * 64, lo:hi] - lim)
            t = jnp.sum(pb.reshape(8, 8, n512), axis=0)
            ls = t if ls is None else ls + t
            Pb[b * 64:(b + 1) * 64, lo:hi] = pb.astype(BF16)
        vv = jnp.concatenate([KV[zz, e, n, 1] for e in range(2) for n in range(2)], axis=1)
        m_acc[B, :, lo:hi] = new
        l_acc[B, :, lo:hi] = l_acc[B, :, lo:hi] * scale + jnp.sum(ls, axis=0, keepdims=True)
        o_acc[B, :, lo:hi] = o_acc[B, :, lo:hi] * scale + jnp.dot(vv, Pb[:, lo:hi], preferred_element_type=F32)

    def ready(zz):
        for n in (0, 1):
            over(zz, n, True).wait_recv()

    def prepare():
        lane = lax.broadcasted_iota(jnp.int32, (1, 512), 1)
        half = lax.rem(lane, 128) // 64
        for j in (0, 1):
            ps = []
            for g in (2 * j, 2 * j + 1):
                gx = x + (g % 2) * (1 - 2 * p)
                gy = ylo + (g // 2) * (1 - 2 * ylo)
                blk = ((z * 2 + gy) * 8 + gx * 2 + c) * 2
                ps.append(jnp.where(half == 0, span[blk], span[blk + 1]))
            qpos[j] = jnp.where(lane < 256, ps[0], ps[1])
        m_acc[...] = jnp.full((4, 1, 512), NEG, F32)
        l_acc[...] = jnp.zeros((4, 1, 512), F32)
        o_acc[...] = jnp.zeros((4, 128, 512), F32)

    def diagonal(pr):
        r = lax.broadcasted_iota(jnp.int32, (128, 256), 0)
        l = lax.rem(lax.broadcasted_iota(jnp.int32, (128, 256), 1), 128)
        ok = jnp.logical_and(r // 64 == l // 64, r <= l)
        sc = jnp.dot(KV[z, c, 0, 0], QB[pr, 0, :, 0:256], preferred_element_type=F32)
        sc = jnp.where(ok, sc, NEG)
        top = jnp.max(sc, axis=0, keepdims=True)
        pb = jnp.where(ok, jnp.exp(sc - top), 0.0)
        m_acc[2 * pr, :, 0:256] = top
        l_acc[2 * pr, :, 0:256] = jnp.sum(pb, axis=0, keepdims=True)
        o_acc[2 * pr, :, 0:256] = jnp.dot(KV[z, c, 0, 1], pb.astype(BF16), preferred_element_type=F32)

    def ocopy(g, pr):
        return rcopy(o_out.at[pr, g - 1], o_in.at[pr, g - 1], o_s.at[0, pr, g - 1], o_r.at[0, pr, g - 1], mate(g))

    def stcopy(g, pr):
        return rcopy(st_out.at[pr, g - 1], st_in.at[pr, g - 1], o_s.at[1, pr, g - 1], o_r.at[1, pr, g - 1], mate(g))

    def give(g, pr):
        B, lo = 2 * pr + g // 2, (g % 2) * 256
        l2 = l_acc[B, :, lo:lo + 256]
        o_out[pr, g - 1] = (o_acc[B, :, lo:lo + 256] * jnp.where(l2 > 0.0, 1.0 / l2, 0.0)).astype(BF16)
        st_out[pr, g - 1, 0:1, :] = m_acc[B, :, lo:lo + 256]
        st_out[pr, g - 1, 1:2, :] = l2
        stcopy(g, pr).start()
        ocopy(g, pr).start()

    def merge(pr):
        for g in (3, 2, 1):
            stcopy(g, pr).wait_recv()
        m0, l0 = m_acc[2 * pr, :, 0:256], l_acc[2 * pr, :, 0:256]
        top = m0
        for g in range(3):
            top = jnp.maximum(top, st_in[pr, g, 0:1, :])
        e0 = jnp.exp(m0 - top)
        ws = [st_in[pr, g, 1:2, :] * jnp.exp(st_in[pr, g, 0:1, :] - top) for g in range(3)]
        inv = 1.0 / (l0 * e0 + ws[0] + ws[1] + ws[2])
        res = o_acc[2 * pr, :, 0:256] * (e0 * inv)
        for g in (3, 2, 1):
            ocopy(g, pr).wait_recv()
        for g in range(3):
            res = res + o_in[pr, g].astype(F32) * (ws[g] * inv)
        for hh in (0, 1):
            h = 2 * pr + hh
            out[0, :, h * 128:(h + 1) * 128] = res[:, hh * 128:(hh + 1) * 128].T.astype(BF16)

    hop(1, (0, 1))
    hop(2, (0, 1))
    each(mm1, 0, 1)
    feed((2,))
    hop(3, (0, 1))
    each(mm1, 1, 3)
    enter((2,))
    hop(4, (0, 1))
    each(mm1, 3, 5)
    hop(1, (2,))
    each(mm1, 5, 8)
    to_sibling(0)
    to_sibling(1)
    hop(2, (2,))
    to_chips(0)
    to_chips(1)
    prepare()
    hop(3, (2,))

    kv = finish(0)
    KV[z, c, 0, 0] = rot(kv[:, :HD]).astype(BF16)
    KV[z, c, 0, 1] = kv[:, HD:].T.astype(BF16)
    for k in (1, 2):
        for i in (0, 1):
            line(i, k).start()
        if k == 1:
            cross(z).start()
            over(z, 0).start()
    hop(4, (2,))
    each(mm2, 0, 3)
    for i in (0, 1):
        arrived(i, 1)
    crossed(z)
    for k in (1, 2):
        for i in (0, 1):
            line1(i, k).start()
    make_queries(0)
    each(mm2, 3, 5)
    for i in (0, 1):
        arrived(i, 2)
    for i in (0, 1):
        line(i, 3).start()
    line(0, 4).start()
    each(mm2, 5, 8)
    to_sibling(2)
    to_chips(2)
    for i in (0, 1):
        arrived1(i, 1)
    diagonal(0)
    for g in (3, 2, 1):
        qcopy(g, 0).wait_recv()

    @functools.partial(lax.fori_loop, 0, 8, init_val=0)
    def _(t, _):
        @pl.when(t == 3)
        def _():
            make_queries(1)

        @pl.when(t == 2)
        def _():
            for i in (0, 1):
                arrived(i, 3)
            arrived(0, 4)

        @pl.when(t == 3)
        def _():
            for i in (0, 1):
                arrived1(i, 2)

        @pl.when(t == 5)
        def _():
            for k in (3, -3, 4):
                crossed(ring8(z + k))
        zz = ring8(z + nth(t))
        ready(zz)
        scores(zz, 1, S0)
        scores(zz, 0, S1)
        soften(zz, 1, S0, P0)
        soften(zz, 0, S1, P1)
        return 0

    for g in (3, 2, 1):
        give(g, 0)
    for g in (3, 2):
        qcopy(g, 1).wait_recv()

    def sweep(B, part=ALL):
        scores(z, B, S0, part)

        @functools.partial(lax.fori_loop, 0, 4, init_val=0)
        def _(t, _):
            za, zb, zc = [ring8(z + nth(lax.rem(2 * t + n, 8))) for n in range(3)]
            scores(zb, B, S1, part)
            soften(za, B, S0, P0, part)
            scores(zc, B, S0, part)
            soften(zb, B, S1, P1, part)
            return 0

    sweep(3)
    give(3, 1)
    give(2, 1)
    qcopy(1, 1).wait_recv()
    sweep(2, (256, 512))
    give(1, 1)
    diagonal(1)
    sweep(2, (0, 256))
    merge(0)
    merge(1)

    for k in (0, 3, -3, 4):
        cross(ring8(z + k)).wait_send()
    for k in (1, 2):
        for i in (0, 1):
            line1(i, k).wait_send()
    @pl.when(src)
    def _():
        for h in (0, 1):
            for n in range(3):
                p1(h, n).wait_send()
    for h in (0, 1):
        for s in (1, -1):
            for k in range(1, hops(s, h) + 1):
                for n in range(3):
                    ring(s, h, k, n).wait_send()
    for part in range(3):
        for j in range(3):
            d2d(j, part).wait_send()
        for pe in (0, 1):
            fin(pe, part).wait_send()
    for pr in (0, 1):
        for g in (1, 2, 3):
            qcopy(g, pr).wait_send()
            ocopy(g, pr).wait_send()
            stcopy(g, pr).wait_send()
    for k in range(1, 5):
        for i in (0, 1):
            if k < 4 or i == 0:
                line(i, k).wait_send()

    @functools.partial(lax.fori_loop, 0, 8, init_val=0)
    def _(t, _):
        for h in (0, 1):
            for n in range(3):
                yout(h, t, n).wait_send()
        for j in range(3):
            xout(t, j).wait_send()
        for n in (0, 1):
            over(t, n).wait_send()
        return 0


def sublayer(tokens, wsh, freq, span):
    dma = pltpu.SemaphoreType.DMA
    vm = pl.BlockSpec(memory_space=pltpu.VMEM)
    return pl.pallas_call(
        sublayer_kernel,
        out_shape=jax.ShapeDtypeStruct((1, 128, 512), BF16),
        in_specs=[pl.BlockSpec(memory_space=pl.ANY)] * 2 + [vm] + [pl.BlockSpec(memory_space=pltpu.SMEM)],
        out_specs=vm,
        scratch_shapes=[
            pltpu.VMEM((8, 512, 384), BF16),
            pltpu.VMEM((16, 384, 256), BF16),
            pltpu.VMEM((16, 384, 128), BF16),
            pltpu.VMEM((3, 768, 256), F32),
            pltpu.VMEM((3, 3, 128, 256), F32),
            pltpu.VMEM((3, 2, 128, 256), F32),
            pltpu.VMEM((3, 2, 128, 256), F32),
            pltpu.VMEM((2, 2, 128, 512), BF16),
            pltpu.VMEM((8, 2, 2, 2, 128, 128), BF16),
            pltpu.VMEM((128, 128), F32),
            pltpu.VMEM((128, 128), F32),
            pltpu.VMEM((512, 512), F32),
            pltpu.VMEM((512, 512), F32),
            pltpu.VMEM((512, 512), BF16),
            pltpu.VMEM((512, 512), BF16),
            pltpu.VMEM((4, 128, 512), F32),
            pltpu.VMEM((4, 1, 512), F32),
            pltpu.VMEM((4, 1, 512), F32),
            pltpu.VMEM((2, 1, 512), jnp.int32),
            pltpu.VMEM((2, 3, 128, 256), BF16),
            pltpu.VMEM((2, 3, 128, 256), BF16),
            pltpu.VMEM((2, 3, 8, 256), F32),
            pltpu.VMEM((2, 3, 8, 256), F32),
            dma((8,)), dma((8, 3)), dma((8, 3)), dma((2,)),
            dma((2, 3)), dma((2, 3)), dma((2, 2, 4, 3)), dma((2, 2, 4, 3)), dma((2, 8, 3)), dma((2, 8, 3)),
            dma((3, 3)), dma((3, 3)), dma((3, 2)), dma((3, 2)),
            dma((2, 3)), dma((2, 3)), dma((2, 4)), dma((2, 4)), dma((2, 2)), dma((2, 2)), dma((8,)), dma((8,)),
            dma((8, 2)), dma((8, 2)), dma((2, 2, 3)), dma((2, 2, 3)),
        ],
        compiler_params=pltpu.CompilerParams(
            collective_id=0, has_side_effects=True, vmem_limit_bytes=56 * 2**20
        ),
    )(tokens, wsh, freq, span)


def per_device(tokens, qkv_weight, span_pos):
    index = np.arange(128, dtype=np.int64)[None, :] % 64
    freq = jnp.asarray((1000000.0 ** (-index * 2.0 / HD)).astype(np.float32))
    return sublayer(tokens, qkv_weight, freq, span_pos)


def solution(mesh):
    in_specs = (P("doc", ("outer", "inner"), None), P("outer", "doc"), P())
    out_specs = P("doc", ("outer", "inner"), None)
    return jax.shard_map(
        per_device, mesh=mesh, in_specs=in_specs, out_specs=out_specs, check_vma=False
    )
```
